256 devices in a mesh: row: 16 (over x_hi, z), col: 16 (over x_lo, y, core).
Axes of the slice: x: 4 (x_hi: 2, x_lo: 2; x = x_hi * 2 + x_lo), y: 4, z: 8, core: 2. Of those that a mesh axis runs over, the one named last changes fastest.
Arguments:
- pair_state: bfloat16 [512, 512, 128], P('row', 'col'), may hold values from -6 to 6
- valid_tokens: int32 [1], replicated, may hold values from 256 to 512
- proj_weight: bfloat16 [128, 512], replicated, may hold values from -0.5 to 0.5
- gate_weight: bfloat16 [128, 128], replicated, may hold values from -0.5 to 0.5
- out_weight: bfloat16 [128, 128], replicated, may hold values from -0.5 to 0.5
- up_weight: bfloat16 [128, 1024], replicated, may hold values from -0.5 to 0.5
- down_weight: bfloat16 [512, 128], replicated, may hold values from -0.25 to 0.25
- gate_scales: float32 [3, 128], replicated, may hold values from 0.5 to 2
- hidden_scales: float32 [512], replicated, may hold values from 0.5 to 2
- cotangent: bfloat16 [512, 512, 128], P('row', 'col'), may hold values from -8 to 8
Outputs:
- layer_out: bfloat16 [512, 512, 128], P('row', 'col')
- gate_grads: float32 [3, 128], replicated
- hidden_grads: float32 [512], replicated
The draws below stay inside these ranges and needn't reach their ends.
All inputs are finite; a program needn't handle non-finite values.
Results may differ from the reference program's by a relative error of at most 0.015.
Values may be sent and summed in bfloat16 or wider, within the bound.
A program may use at most 128 MiB of HBM per device.

```python
import math
import jax
import jax.numpy as jnp
from jax import lax

C = 128
FF = 512
TOK_BLK = 32
N = 512
N_ROW = 16


def draw_cotangent(key, part):
    key = jax.random.fold_in(key, 11)
    first_index = jnp.arange(N, dtype=jnp.float32)[:, None, None]
    second_index = jnp.arange(N, dtype=jnp.float32)[None, :, None]
    position_ramp = (first_index + second_index) / N
    samples = jnp.clip(jax.random.normal(key, (N, N, C), jnp.float32), -3.5, 3.5)
    growth = 3.0 ** position_ramp
    return (0.05 * samples * growth).astype(jnp.bfloat16)


def block_levels(key, dims, pieces, low, largest):
    level, own = 1.0, jax.random.fold_in(key, 6)
    for dim, blocks in pieces:
        heights = jnp.exp(jax.random.uniform(jax.random.fold_in(own, dim), (blocks,), jnp.float32, low / len(pieces), largest / len(pieces)))
        level = level * jnp.repeat(heights, dims[dim] // blocks).reshape([-1 if axis == dim else 1 for axis in range(len(dims))])
    return level


def bell_draw(key, dims, spread, limit, pieces=(), kind=jnp.bfloat16):
    values = spread * jax.random.normal(key, dims, jnp.float32)
    if pieces:
        values = values * block_levels(key, dims, pieces, -0.22, 0.18)
    return jnp.clip(values, -limit, limit).astype(kind)


def setup_inputs(seed: int = 0) -> dict:
    keys = jax.random.split(jax.random.key(seed), 11)
    return {
        "pair_state": bell_draw(keys[0], (N, N, C), 1.0, 6.0, ((0, 16), (1, 16))),
        "valid_tokens": jax.random.randint(keys[1], (1,), N // 2, N + 1).astype(jnp.int32),
        "proj_weight": bell_draw(keys[2], (C, 4 * C), C ** -0.5, 0.5),
        "gate_weight": bell_draw(keys[3], (C, C), C ** -0.5, 0.5),
        "out_weight": bell_draw(keys[4], (C, C), C ** -0.5, 0.5),
        "up_weight": bell_draw(keys[5], (C, 2 * FF), C ** -0.5, 0.5),
        "down_weight": bell_draw(keys[6], (FF, C), FF ** -0.5, 0.25),
        "gate_scales": jnp.clip(jnp.exp(jax.random.uniform(keys[7], (3, C), jnp.float32, math.log(0.5), math.log(2.0))), 0.5, 2.0),
        "hidden_scales": jnp.clip(jnp.exp(jax.random.uniform(keys[8], (FF,), jnp.float32, math.log(0.5), math.log(2.0))), 0.5, 2.0),
        "cotangent": draw_cotangent(jax.random.fold_in(keys[10], 71), 0),
    }


epsilon = 1e-05

def layer_norm(values):
    average = lax.optimization_barrier(jnp.mean(values, axis=-1, keepdims=True))
    centred = values - average
    inverse_std = lax.rsqrt(lax.optimization_barrier(jnp.mean(centred * centred, axis=-1, keepdims=True)) + epsilon)
    return (centred * inverse_std, inverse_std)

def norm_backward(gradient, normed, inverse_std):
    grad_mean = lax.optimization_barrier(jnp.mean(gradient, axis=-1, keepdims=True))
    cross_mean = lax.optimization_barrier(jnp.mean(gradient * normed, axis=-1, keepdims=True))
    return inverse_std * (gradient - grad_mean - normed * cross_mean)

def linear_map(values, weight):
    flattened = values.reshape(-1, values.shape[-1])
    result = jnp.dot(flattened, weight, preferred_element_type=jnp.float32)
    return result.reshape(values.shape[:-1] + (weight.shape[1],))

def linear_back(values, weight):
    flattened = values.reshape(-1, values.shape[-1])
    result = jnp.dot(flattened, weight.T, preferred_element_type=jnp.float32)
    return result.reshape(values.shape[:-1] + (weight.shape[0],))

def project_inputs(pair_state, pair_mask, proj_weight, gate_weight, gate_scales):
    channels = pair_state.shape[-1]
    normed = layer_norm(pair_state.astype(jnp.float32))[0].astype(jnp.bfloat16)
    projected = linear_map(normed, proj_weight)
    value_left = projected[..., :channels]
    value_right = projected[..., channels:2 * channels]
    logit_left = projected[..., 2 * channels:3 * channels]
    logit_right = projected[..., 3 * channels:]
    sigma_left = jax.nn.sigmoid(gate_scales[0] * logit_left)
    sigma_right = jax.nn.sigmoid(gate_scales[1] * logit_right)
    left_proj = (pair_mask * sigma_left * value_left).astype(jnp.bfloat16)
    right_proj = (pair_mask * sigma_right * value_right).astype(jnp.bfloat16)
    left_slope = (pair_mask * value_left * sigma_left * (1.0 - sigma_left) * logit_left).astype(jnp.bfloat16)
    right_slope = (pair_mask * value_right * sigma_right * (1.0 - sigma_right) * logit_right).astype(jnp.bfloat16)
    gate_logit = linear_map(normed, gate_weight)
    gate_value = jax.nn.sigmoid(gate_scales[2] * gate_logit)
    return (left_proj, right_proj, left_slope, right_slope, gate_logit, gate_value)

def finish(pair_state, triangle, gate_logit, gate_value, out_weight, up_weight, down_weight, hidden_scales, cotangent):
    tri_hat, tri_inverse = layer_norm(triangle)
    tri_normed = tri_hat.astype(jnp.bfloat16)
    out_proj = linear_map(tri_normed, out_weight)
    middle = (pair_state.astype(jnp.float32) + gate_value * out_proj).astype(jnp.bfloat16)
    middle = lax.optimization_barrier(middle)
    middle_full = middle.astype(jnp.float32)
    mid_hat, mid_inverse = layer_norm(middle_full)
    mid_normed = mid_hat.astype(jnp.bfloat16)
    upward = linear_map(mid_normed, up_weight)
    hidden_width = hidden_scales.shape[0]
    first_half = upward[..., :hidden_width]
    second_half = upward[..., hidden_width:]
    activated = jax.nn.silu(first_half)
    product = activated * second_half
    hidden = (hidden_scales * product).astype(jnp.bfloat16)
    layer_out = (middle_full + linear_map(hidden, down_weight)).astype(jnp.bfloat16)
    hidden_grad = linear_back(cotangent, down_weight)
    hidden_term = lax.optimization_barrier(jnp.sum(hidden_grad * product, axis=(0, 1)))
    sigma_first = jax.nn.sigmoid(first_half)
    scaled = hidden_grad * hidden_scales
    grad_first = scaled * second_half * sigma_first * (1.0 + first_half * (1.0 - sigma_first))
    grad_second = scaled * activated
    grad_upward = jnp.concatenate([grad_first, grad_second], axis=-1).astype(jnp.bfloat16)
    grad_mid = cotangent.astype(jnp.float32) + norm_backward(linear_back(grad_upward, up_weight), mid_hat, mid_inverse)
    gate_term = lax.optimization_barrier(jnp.sum(grad_mid * out_proj * gate_value * (1.0 - gate_value) * gate_logit, axis=(0, 1)))
    grad_outproj = (grad_mid * gate_value).astype(jnp.bfloat16)
    triangle_grad = norm_backward(linear_back(grad_outproj, out_weight), tri_hat, tri_inverse).astype(jnp.bfloat16)
    return (layer_out, triangle_grad, gate_term, hidden_term)

def reference(pair_state, valid_tokens, proj_weight, gate_weight, out_weight, up_weight, down_weight, gate_scales, hidden_scales, cotangent):
    positions = jnp.arange(N, dtype=jnp.int32)
    keep = (positions < valid_tokens[0]).astype(jnp.float32)
    pair_mask = keep[:, None, None] * keep[None, :, None]

    def front_block(block_items):
        return project_inputs(block_items[0], block_items[1], proj_weight, gate_weight, gate_scales)
    blocked = lax.map(front_block, (pair_state.reshape(N_ROW, TOK_BLK, N, C), pair_mask.reshape(N_ROW, TOK_BLK, N, 1)))
    outputs = [stacked.reshape((N, N) + stacked.shape[3:]) for stacked in blocked]
    left_proj, right_proj, left_slope, right_slope, gate_logit, gate_value = outputs
    triangle = jnp.einsum('ikc,jkc->ijc', left_proj.astype(jnp.float32), right_proj.astype(jnp.float32), precision=lax.Precision.HIGHEST)

    def back_block(block_items):
        return finish(block_items[0], block_items[1], block_items[2], block_items[3], out_weight, up_weight, down_weight, hidden_scales, block_items[4])

    def split_rows(values):
        return values.reshape((N_ROW, TOK_BLK) + values.shape[1:])
    layer_out, triangle_grad, gate_term, hidden_term = lax.map(back_block, (split_rows(pair_state), split_rows(triangle), split_rows(gate_logit), split_rows(gate_value), split_rows(cotangent)))
    layer_out = layer_out.reshape(N, N, C)
    triangle_grad = triangle_grad.reshape(N, N, C).astype(jnp.float32)
    grad_left = jnp.einsum('ijc,jkc->ikc', triangle_grad, right_proj.astype(jnp.float32), precision=lax.Precision.HIGHEST)
    left_term = lax.optimization_barrier(jnp.sum(grad_left * left_slope.astype(jnp.float32), axis=(0, 1)))
    grad_right = jnp.einsum('ijc,ikc->jkc', triangle_grad, left_proj.astype(jnp.float32), precision=lax.Precision.HIGHEST)
    right_term = lax.optimization_barrier(jnp.sum(grad_right * right_slope.astype(jnp.float32), axis=(0, 1)))
    gate_grads = jnp.stack([left_term, right_term, lax.optimization_barrier(jnp.sum(gate_term, axis=0))])
    hidden_grads = lax.optimization_barrier(jnp.sum(hidden_term, axis=0))
    return (layer_out, gate_grads, hidden_grads)
```

```python
import functools

import jax
import jax.numpy as jnp
from jax import lax
from jax.experimental import pallas as pl
from jax.experimental.pallas import tpu as pltpu
from jax.sharding import PartitionSpec as P

F32, BF16 = jnp.float32, jnp.bfloat16
EPS = 1e-5
MESH = pl.DeviceIdType.MESH
C = 128
BLK = 32
SA = 65
ST = 33


def mm(a, b):
    return jnp.dot(a, b, preferred_element_type=F32)


def mm_nt(a, b):
    return lax.dot_general(a, b, (((1,), (1,)), ((), ())), preferred_element_type=F32)


def sigmoid(v):
    return 0.5 * jnp.tanh(0.5 * v) + 0.5


def norm(v):
    centred = v - jnp.mean(v, axis=-1, keepdims=True)
    inverse = lax.rsqrt(jnp.mean(centred * centred, axis=-1, keepdims=True) + EPS)
    return centred * inverse, inverse


def norm_back(g, hat, inverse):
    g_mean = jnp.mean(g, axis=-1, keepdims=True)
    cross = jnp.mean(g * hat, axis=-1, keepdims=True)
    return inverse * (g - g_mean - hat * cross)


class Copies:
    def __init__(self, send, recv):
        self.send, self.recv, self.count, self.table = send, recv, 0, {}

    def start(self, name, src, dst, device, when=None):
        copy = pltpu.make_async_remote_copy(
            src_ref=src,
            dst_ref=dst,
            send_sem=self.send.at[self.count],
            recv_sem=self.recv.at[self.count],
            device_id=device,
            device_id_type=MESH,
        )
        self.count += 1
        self.table[name] = (copy, when)
        if when is None:
            copy.start()
        else:
            pl.when(when)(copy.start)

    def wait_recv(self, name):
        copy, when = self.table[name]
        if when is None:
            copy.wait_recv()
        else:
            pl.when(when)(copy.wait_recv)

    def wait_sends(self):
        for copy, when in self.table.values():
            if when is None:
                copy.wait_send()
            else:
                pl.when(when)(copy.wait_send)


N_COPIES = 47


def project(pan, blocks, quad, w_ref, s_ref, out):
    def step(n, carry):
        i = n * 2
        x = jnp.concatenate([pan[b, i + m] for m in range(2) for b in blocks], axis=0)
        p = mm_nt(w_ref[...], x)
        for m in range(2):
            value, logit = p[:C, m * 128 : (m + 1) * 128], p[C:, m * 128 : (m + 1) * 128]
            sig = 0.5 * jnp.tanh(s_ref[...] * logit) + 0.5
            proj = sig * value
            slope = proj * (logit * (1.0 - sig))
            out[quad, pl.ds(i + m, C, stride=SA), :] = proj
            out[quad, pl.ds(i + m + BLK, C, stride=SA), :] = slope
        return carry

    lax.fori_loop(0, BLK // 2, step, 0)


def products(a_ref, b_ref, t_ref):
    def step(n, carry):
        for m in range(4):
            ch = n * 4 + m
            rows = pl.ds(ch * SA, 2 * BLK)
            a = jnp.concatenate([a_ref[q, rows, :].astype(BF16) for q in range(4)], axis=1)
            b = jnp.concatenate([b_ref[q, rows, :].astype(BF16) for q in range(4)], axis=1)
            t = mm_nt(a, b)
            t_ref[pl.ds(ch * ST, BLK), :] = jnp.concatenate([t[:BLK], t[BLK:]], axis=1)
        return carry

    lax.fori_loop(0, C // 4, step, 0)


def finish(x_ref, cot_ref, gate_w, out_w, up_w, down_w, gs_ref, hs_ref, t_ref, out_ref, vec_ref, tri, tri_l, tri_r, acc):
    def turn(i, carry):
        t = t_ref[pl.ds(i, C, stride=ST), :].T
        rows = pl.ds(pl.multiple_of(i * BLK, BLK), BLK)
        tri[rows, :] = t[:BLK]
        tri_r[rows, :] = t[BLK : 2 * BLK]
        tri_l[rows, :] = t[2 * BLK : 3 * BLK]
        return carry

    lax.fori_loop(0, BLK, turn, 0)
    acc[...] = jnp.zeros_like(acc)
    n_rows = 8
    n_pos = n_rows * BLK
    gs = gs_ref[2:3, :]
    hs = hs_ref[...]

    def chunk(n, carry):
        own = pl.ds(n * n_rows, n_rows)
        rows = pl.ds(pl.multiple_of(n * n_pos, n_pos), n_pos)
        x = x_ref[own].reshape(n_pos, C).astype(F32)
        cot = cot_ref[own].reshape(n_pos, C)
        gate_logit = mm(norm(x)[0].astype(BF16), gate_w[...])
        gate = sigmoid(gs * gate_logit)
        tri_hat, tri_inv = norm(tri[rows, :])
        out_proj = mm(tri_hat.astype(BF16), out_w[...])
        middle = (x + gate * out_proj).astype(BF16).astype(F32)
        mid_hat, mid_inv = norm(middle)
        upward = mm(mid_hat.astype(BF16), up_w[...])
        first, second = upward[:, :512], upward[:, 512:]
        s = sigmoid(first)
        act = first * s
        product = act * second
        layer_out = middle + mm((hs * product).astype(BF16), down_w[...])
        out_ref[own] = layer_out.astype(BF16).reshape(n_rows, BLK, C)
        hidden_grad = mm_nt(cot, down_w[...])
        hidden = jnp.sum(hidden_grad * product, axis=0, keepdims=True)
        scaled = hidden_grad * hs
        g_first = scaled * second * s * (1.0 + first * (1.0 - s))
        g_second = scaled * act
        g_up = jnp.concatenate([g_first.astype(BF16), g_second.astype(BF16)], axis=1)
        g_mid = cot.astype(F32) + norm_back(mm_nt(g_up, up_w[...]), mid_hat, mid_inv)
        gate_term = jnp.sum(g_mid * out_proj * gate * (1.0 - gate) * gate_logit, axis=0, keepdims=True)
        g_out = (g_mid * gate).astype(BF16)
        t_grad = norm_back(mm_nt(g_out, out_w[...]), tri_hat, tri_inv).astype(BF16).astype(F32)
        left = jnp.sum(t_grad * tri_l[rows, :], axis=0, keepdims=True)
        right = jnp.sum(t_grad * tri_r[rows, :], axis=0, keepdims=True)
        parts = [left, right, gate_term] + [hidden[:, m * C : (m + 1) * C] for m in range(4)]
        for m, part in enumerate(parts):
            acc[m : m + 1, :] += part
        return carry

    lax.fori_loop(0, BLK // n_rows, chunk, 0)
    vec_ref[...] = acc[...]


def layer_kernel(
    x_ref, valid_ref, proj_w, gate_w, out_w, up_w, down_w, gs_ref, hs_ref, cot_ref,
    out_ref, vec_ref,
    lpan, rpan, a_ref, b_ref, t_ref, tri, tri_l, tri_r, acc, wa, wb, sa, sb, send, recv,
):
    r, c = lax.axis_index("row"), lax.axis_index("col")
    xh, z = r // 8, r % 8
    xl, y, core = c // 8, (c // 2) % 4, c % 2

    def row_of(h, dz):
        return h * 8 + (z + dz) % 8

    def col_of(h, dy, k):
        return (h * 4 + (y + dy) % 4) * 2 + k

    across = (c, r)
    far = (row_of(1 - xh, 0), c)
    up, down = (row_of(xh, 1), c), (row_of(xh, 7), c)
    sibling = (r, col_of(xl, 0, 1 - core))
    near = (r, col_of(1 - xl, 0, core))
    along = [(r, col_of(xl, d, core)) for d in (1, 2, 3)]
    off = r != c

    barrier = pltpu.get_barrier_semaphore()
    partners = [far, up, down, sibling, near] + along
    for device in partners:
        pl.semaphore_signal(barrier, inc=1, device_id=device, device_id_type=MESH)

    @pl.when(off)
    def _():
        pl.semaphore_signal(barrier, inc=1, device_id=across, device_id_type=MESH)

    limit = valid_ref[0]
    rows_i = lax.broadcasted_iota(jnp.int32, (BLK, BLK, C), 0) + r * BLK
    rows_k = lax.broadcasted_iota(jnp.int32, (BLK, BLK, C), 1) + c * BLK
    keep = jnp.where(jnp.maximum(rows_i, rows_k) < limit, 1.0, 0.0)
    normed = (norm(x_ref[...].astype(F32))[0] * keep).astype(BF16)
    lpan[c] = normed

    @pl.when(jnp.logical_not(off))
    def _():
        rpan[r] = normed

    pl.semaphore_wait(barrier, len(partners) + jnp.where(off, 1, 0))

    cp = Copies(send, recv)
    halves = (pl.ds(0, 16), pl.ds(16, 16))

    def r_copy(name, slot, half, device):
        ref = rpan.at[slot, halves[half]]
        cp.start(name, ref, ref, device)

    def l_copy(name, slot, device):
        ref = lpan.at[slot]
        cp.start(name, ref, ref, device)

    for half in range(2):
        cp.start(("t", half), lpan.at[c, halves[half]], rpan.at[c, halves[half]], across, off)
    l_copy("near", c, near)
    for d in range(3):
        l_copy(("y", d, 0), c, along[d])
    l_copy("sib", c, sibling)

    for w_ref, s_ref, side in ((wa, sa, 0), (wb, sb, 1)):
        w_ref[:C, :] = proj_w[:, side * C : (side + 1) * C].T
        w_ref[C:, :] = proj_w[:, (side + 2) * C : (side + 3) * C].T
        s_ref[...] = jnp.broadcast_to(0.5 * gs_ref[side : side + 1, :], (C, C)).T

    for half in range(2):
        cp.wait_recv(("t", half))
        r_copy(("up", 1, half), r, half, up)
        r_copy(("down", 1, half), r, half, down)
        r_copy(("far", half), r, half, far)
    cp.wait_recv("near")
    for d in range(3):
        l_copy(("y", d, 1), col_of(1 - xl, 0, core), along[d])
    l_copy("sibnear", col_of(1 - xl, 0, core), sibling)
    cp.wait_recv(("far", 0))
    r_copy(("up", 1, 2), row_of(1 - xh, 0), 0, up)
    r_copy(("down", 1, 2), row_of(1 - xh, 0), 0, down)

    items = {"up": {1: (0, 1, 2), 2: (0, 1, 2), 3: (0, 1, 2), 4: (0, 2)}, "down": {1: (0, 1, 2), 2: (0, 1, 2), 3: (0, 1, 2), 4: (1,)}}

    def hop(h):
        for item in range(3):
            for flow, sign, device in (("up", -1, up), ("down", 1, down)):
                if item not in items[flow][h]:
                    continue
                cp.wait_recv((flow, h, item))
                slot = row_of(1 - xh if item == 2 else xh, sign * h + 8)
                if h < 4 and item in items[flow][h + 1]:
                    r_copy((flow, h + 1, item), slot, item % 2, device)
                if item == 1:
                    r_copy(("cross", flow, h), slot, 1, far)

    def l_hop(part):
        for d in range(3):
            cp.wait_recv(("y", d, part))
            slot = col_of(1 - xl if part else xl, 3 - d, core)
            l_copy(("sib", d, part), slot, sibling)

    hop(1)
    l_hop(0)
    hop(2)
    l_hop(1)
    for name in ["sib", "sibnear"] + [("sib", d, part) for part in range(2) for d in range(3)]:
        cp.wait_recv(name)
    hop(3)
    hop(4)
    cp.wait_recv(("far", 1))
    for flow, last in (("up", 3), ("down", 4)):
        for h in range(1, last + 1):
            cp.wait_recv(("cross", flow, h))

    order = [0, 7, 1, 6, 2, 5, 3, 4]
    quads = [[row_of(h, dz) for dz in order[2 * q : 2 * q + 2] for h in range(2)] for q in range(4)]
    for q in range(4):
        project(lpan, quads[q], q, wa, sa, a_ref)
        project(rpan, quads[q], q, wb, sb, b_ref)
    products(a_ref, b_ref, t_ref)
    finish(x_ref, cot_ref, gate_w, out_w, up_w, down_w, gs_ref, hs_ref, t_ref, out_ref, vec_ref, tri, tri_l, tri_r, acc)
    cp.wait_sends()
    assert cp.count == N_COPIES


def sum_kernel(v_ref, o_ref, slots, send, recv):
    r, c = lax.axis_index("row"), lax.axis_index("col")
    xh, z = r // 8, r % 8
    xl, y, core = c // 8, (c // 2) % 4, c % 2
    line = [((xh * 8 + (z + dz) % 8), (c // 2) * 2 + (core + dk) % 2) for dz in range(8) for dk in range(2)]
    plane = [
        (((xh + dh) % 2) * 8 + z, (((xl + dl) % 2) * 4 + (y + dy) % 4) * 2 + core)
        for dh in range(2) for dl in range(2) for dy in range(4)
    ]
    places = (z * 2 + core, (xh * 2 + xl) * 4 + y)
    barrier = pltpu.get_barrier_semaphore()
    for device in line[1:] + plane[1:]:
        pl.semaphore_signal(barrier, inc=1, device_id=device, device_id_type=MESH)
    pl.semaphore_wait(barrier, 30)
    total = v_ref[...]
    for stage, group in enumerate((line, plane)):
        slots[stage, places[stage]] = total
        copies = []
        for n in range(1, 16):
            copy = pltpu.make_async_remote_copy(
                src_ref=slots.at[stage, places[stage]],
                dst_ref=slots.at[stage, places[stage]],
                send_sem=send.at[stage, n],
                recv_sem=recv.at[stage, n],
                device_id=group[n],
                device_id_type=MESH,
            )
            copy.start()
            copies.append(copy)
        for copy in copies:
            copy.wait()
        total = jnp.sum(slots[stage], axis=0)
    o_ref[...] = total


VMEM = pl.BlockSpec(memory_space=pltpu.VMEM)
SMEM = pl.BlockSpec(memory_space=pltpu.SMEM)


def shards(pair_state, valid_tokens, proj_weight, gate_weight, out_weight, up_weight, down_weight, gate_scales, hidden_scales, cotangent):
    panel = pltpu.VMEM((16, BLK, BLK, C), BF16)
    edge = pltpu.VMEM((4, C * SA, 128), F32)
    positions = pltpu.VMEM((BLK * BLK, C), F32)
    layer_out, vector = pl.pallas_call(
        layer_kernel,
        out_shape=(jax.ShapeDtypeStruct((BLK, BLK, C), BF16), jax.ShapeDtypeStruct((8, C), F32)),
        in_specs=[VMEM, SMEM] + [VMEM] * 8,
        out_specs=(VMEM, VMEM),
        scratch_shapes=[
            panel, panel, edge, edge, pltpu.VMEM((C * ST, 128), F32), positions, positions, positions,
            pltpu.VMEM((8, C), F32), pltpu.VMEM((2 * C, C), BF16), pltpu.VMEM((2 * C, C), BF16),
            pltpu.VMEM((C, C), F32), pltpu.VMEM((C, C), F32),
            pltpu.SemaphoreType.DMA((N_COPIES,)), pltpu.SemaphoreType.DMA((N_COPIES,)),
        ],
        compiler_params=pltpu.CompilerParams(collective_id=0, has_side_effects=True, vmem_limit_bytes=60 << 20),
        name="layer",
    )(pair_state, valid_tokens, proj_weight, gate_weight, out_weight, up_weight, down_weight, gate_scales, hidden_scales.reshape(1, 512), cotangent)
    total = pl.pallas_call(
        sum_kernel,
        out_shape=jax.ShapeDtypeStruct((8, C), F32),
        in_specs=[VMEM],
        out_specs=VMEM,
        scratch_shapes=[pltpu.VMEM((2, 16, 8, C), F32), pltpu.SemaphoreType.DMA((2, 16)), pltpu.SemaphoreType.DMA((2, 16))],
        compiler_params=pltpu.CompilerParams(collective_id=1, has_side_effects=True),
        name="sums",
    )(vector)
    return layer_out, total[:3], total[3:7].reshape(512)


def solution(mesh):
    return jax.shard_map(
        shards,
        mesh=mesh,
        in_specs=(P("row", "col", None), P(), P(), P(), P(), P(), P(), P(), P(), P("row", "col", None)),
        out_specs=(P("row", "col", None), P(), P()),
        check_vma=False,
    )
```

```python
import functools

import jax
import jax.numpy as jnp
from jax import lax
from jax.experimental import pallas as pl
from jax.experimental.pallas import tpu as pltpu
from jax.sharding import PartitionSpec as P

F32, BF16 = jnp.float32, jnp.bfloat16
EPS = 1e-5
MESH = pl.DeviceIdType.MESH
C = 128
BLK = 32
SA = 65
GROUP = 16
WIDE = 32
ST = 33


def mm(a, b):
    return jnp.dot(a, b, preferred_element_type=F32)


def mm_nt(a, b):
    return lax.dot_general(a, b, (((1,), (1,)), ((), ())), preferred_element_type=F32)


def sigmoid(v):
    return 0.5 * jnp.tanh(0.5 * v) + 0.5


def norm(v):
    centred = v - jnp.mean(v, axis=-1, keepdims=True)
    inverse = lax.rsqrt(jnp.mean(centred * centred, axis=-1, keepdims=True) + EPS)
    return centred * inverse, inverse


def norm_back(g, hat, inverse):
    g_mean = jnp.mean(g, axis=-1, keepdims=True)
    cross = jnp.mean(g * hat, axis=-1, keepdims=True)
    return inverse * (g - g_mean - hat * cross)


class Copies:
    def __init__(self, send, recv):
        self.send, self.recv, self.count, self.table = send, recv, 0, {}

    def start(self, name, src, dst, device, when=None):
        copy = pltpu.make_async_remote_copy(
            src_ref=src,
            dst_ref=dst,
            send_sem=self.send.at[self.count],
            recv_sem=self.recv.at[self.count],
            device_id=device,
            device_id_type=MESH,
        )
        self.count += 1
        self.table[name] = (copy, when)
        if when is None:
            copy.start()
        else:
            pl.when(when)(copy.start)

    def wait_recv(self, name):
        copy, when = self.table[name]
        if when is None:
            copy.wait_recv()
        else:
            pl.when(when)(copy.wait_recv)

    def wait_sends(self):
        for copy, when in self.table.values():
            if when is None:
                copy.wait_send()
            else:
                pl.when(when)(copy.wait_send)


N_COPIES = 47


def project(pan, blocks, quad, w_ref, s_ref, out):
    def step(n, carry):
        i = n * GROUP
        x = jnp.concatenate([pan[b, i + m] for m in range(GROUP) for b in blocks], axis=0)
        p = mm_nt(w_ref[...], x)
        for m in range(GROUP):
            value, logit = p[:C, m * 128 : (m + 1) * 128], p[C:, m * 128 : (m + 1) * 128]
            sig = 0.5 * jnp.tanh(s_ref[...] * logit) + 0.5
            proj = sig * value
            slope = proj * (logit * (1.0 - sig))
            out[quad, pl.ds(i + m, C, stride=SA), :] = proj
            out[quad, pl.ds(i + m + BLK, C, stride=SA), :] = slope
        return carry

    lax.fori_loop(0, BLK // GROUP, step, 0)


def products(a_ref, b_ref, t_ref):
    def step(n, carry):
        for m in range(WIDE):
            ch = n * WIDE + m
            rows = pl.ds(ch * SA, 2 * BLK)
            a = jnp.concatenate([a_ref[q, rows, :].astype(BF16) for q in range(4)], axis=1)
            b = jnp.concatenate([b_ref[q, rows, :].astype(BF16) for q in range(4)], axis=1)
            t = mm_nt(a, b)
            t_ref[pl.ds(ch * ST, BLK), :] = jnp.concatenate([t[:BLK], t[BLK:]], axis=1)
        return carry

    lax.fori_loop(0, C // WIDE, step, 0)


N_ROWS = 16
N_POS = N_ROWS * BLK


def parts_of(n):
    return pl.ds(n * N_ROWS, N_ROWS), pl.ds(pl.multiple_of(n * N_POS, N_POS), N_POS)


def early(x_ref, cot_ref, gate_w, down_w, gs_ref, logit_ref, gate_ref, hg_ref):
    gs = gs_ref[2:3, :]

    def chunk(n, carry):
        own, rows = parts_of(n)
        x = x_ref[own].reshape(N_POS, C).astype(F32)
        gate_logit = mm(norm(x)[0].astype(BF16), gate_w[...])
        logit_ref[rows, :] = gate_logit
        gate_ref[rows, :] = sigmoid(gs * gate_logit)
        hg_ref[rows, :] = mm_nt(cot_ref[own].reshape(N_POS, C), down_w[...])
        return carry

    lax.fori_loop(0, BLK // N_ROWS, chunk, 0)


def turn(t_ref, tri, tri_l, tri_r):
    def step(n, carry):
        for m in range(4):
            i = n * 4 + m
            t = t_ref[pl.ds(i, C, stride=ST), :].T
            rows = pl.ds(pl.multiple_of(i * BLK, BLK), BLK)
            tri[rows, :] = t[:BLK]
            tri_r[rows, :] = t[BLK : 2 * BLK]
            tri_l[rows, :] = t[2 * BLK : 3 * BLK]
        return carry

    lax.fori_loop(0, BLK // 4, step, 0)


def finish(x_ref, cot_ref, out_w, up_w, down_w, hs_ref, logit_ref, gate_ref, hg_ref, tri, tri_l, tri_r, out_ref, acc):
    acc[...] = jnp.zeros_like(acc)
    hs = hs_ref[...]

    def chunk(n, carry):
        own, rows = parts_of(n)
        x = x_ref[own].reshape(N_POS, C).astype(F32)
        cot = cot_ref[own].reshape(N_POS, C).astype(F32)
        gate_logit, gate, hidden_grad = logit_ref[rows, :], gate_ref[rows, :], hg_ref[rows, :]
        tri_hat, tri_inv = norm(tri[rows, :])
        out_proj = mm(tri_hat.astype(BF16), out_w[...])
        middle = (x + gate * out_proj).astype(BF16).astype(F32)
        mid_hat, mid_inv = norm(middle)
        upward = mm(mid_hat.astype(BF16), up_w[...])
        first, second = upward[:, :512], upward[:, 512:]
        s = sigmoid(first)
        act = first * s
        product = act * second
        layer_out = middle + mm((hs * product).astype(BF16), down_w[...])
        out_ref[own] = layer_out.astype(BF16).reshape(N_ROWS, BLK, C)
        hidden = jnp.sum(hidden_grad * product, axis=0, keepdims=True)
        scaled = hidden_grad * hs
        g_first = scaled * second * s * (1.0 + first * (1.0 - s))
        g_second = scaled * act
        g_up = jnp.concatenate([g_first.astype(BF16), g_second.astype(BF16)], axis=1)
        g_mid = cot + norm_back(mm_nt(g_up, up_w[...]), mid_hat, mid_inv)
        gate_term = jnp.sum(g_mid * out_proj * gate * (1.0 - gate) * gate_logit, axis=0, keepdims=True)
        g_out = (g_mid * gate).astype(BF16)
        t_grad = norm_back(mm_nt(g_out, out_w[...]), tri_hat, tri_inv).astype(BF16).astype(F32)
        left = jnp.sum(t_grad * tri_l[rows, :], axis=0, keepdims=True)
        right = jnp.sum(t_grad * tri_r[rows, :], axis=0, keepdims=True)
        parts = [left, right, gate_term] + [hidden[:, m * C : (m + 1) * C] for m in range(4)]
        for m, part in enumerate(parts):
            acc[m : m + 1, :] += part
        return carry

    lax.fori_loop(0, BLK // N_ROWS, chunk, 0)


def layer_kernel(
    x_ref, valid_ref, proj_w, gate_w, out_w, up_w, down_w, gs_ref, hs_ref, cot_ref,
    out_ref, gate_out, hidden_out,
    lpan, rpan, a_ref, b_ref, t_ref, tri, tri_l, tri_r, logit_ref, gate_ref, hg_ref, acc, wa, wb, sa, sb, slots,
    send, recv, sum_send, sum_recv,
):
    r, c = lax.axis_index("row"), lax.axis_index("col")
    xh, z = r // 8, r % 8
    xl, y, core = c // 8, (c // 2) % 4, c % 2

    def row_of(h, dz):
        return h * 8 + (z + dz) % 8

    def col_of(h, dy, k):
        return (h * 4 + (y + dy) % 4) * 2 + k

    def slot_of(h, dz):
        return h * 8 + (z + dz + 8 - c % 8) % 8

    def col_at(slot):
        return slot // 8 * 8 + slot % 4 * 2 + slot % 8 // 4

    own_slot = slot_of(xh, 0)
    to = (xl * 8 + (z + y + 4 * core) % 8, r)
    sent_slot = xl * 8 + y + 4 * core
    source = (c, col_at(own_slot))
    off = jnp.logical_or(c != r, own_slot % 8 != sent_slot % 8)

    far = (row_of(1 - xh, 0), c)
    up, down = (row_of(xh, 1), c), (row_of(xh, 7), c)
    sibling = (r, col_of(xl, 0, 1 - core))
    near = (r, col_of(1 - xl, 0, core))
    along = [(r, col_of(xl, d, core)) for d in (1, 2, 3)]
    line = [(row_of(xh, dz), col_of(xl, 0, (core + dk) % 2)) for dz in range(8) for dk in range(2)]
    plane = [
        (row_of((xh + dh) % 2, 0), col_of((xl + dl) % 2, dy, core))
        for dh in range(2) for dl in range(2) for dy in range(4)
    ]

    barrier = pltpu.get_barrier_semaphore()
    for device in line[1:] + plane[1:]:
        pl.semaphore_signal(barrier, inc=1, device_id=device, device_id_type=MESH)

    @pl.when(off)
    def _():
        pl.semaphore_signal(barrier, inc=1, device_id=source, device_id_type=MESH)

    limit = valid_ref[0]
    rows_i = lax.broadcasted_iota(jnp.int32, (BLK, BLK, C), 0) + r * BLK
    rows_k = lax.broadcasted_iota(jnp.int32, (BLK, BLK, C), 1) + c * BLK
    keep = jnp.where(jnp.maximum(rows_i, rows_k) < limit, 1.0, 0.0)
    normed = (norm(x_ref[...].astype(F32))[0] * keep).astype(BF16)
    lpan[c] = normed

    @pl.when(jnp.logical_not(off))
    def _():
        rpan[own_slot] = normed

    pl.semaphore_wait(barrier, 30 + jnp.where(off, 1, 0))

    cp = Copies(send, recv)
    halves = (pl.ds(0, 16), pl.ds(16, 16))

    def r_copy(name, slot, half, device):
        ref = rpan.at[slot, halves[half]]
        cp.start(name, ref, ref, device)

    def l_copy(name, slot, device):
        ref = lpan.at[slot]
        cp.start(name, ref, ref, device)

    for half in (1, 0):
        cp.start(("t", half), lpan.at[c, halves[half]], rpan.at[sent_slot, halves[half]], to, off)
    l_copy("near", c, near)
    for d in range(3):
        l_copy(("y", d, 0), c, along[d])
    l_copy("sib", c, sibling)

    for w_ref, s_ref, side in ((wa, sa, 0), (wb, sb, 1)):
        w_ref[:C, :] = proj_w[:, side * C : (side + 1) * C].T
        w_ref[C:, :] = proj_w[:, (side + 2) * C : (side + 3) * C].T
        s_ref[...] = jnp.broadcast_to(0.5 * gs_ref[side : side + 1, :], (C, C)).T
    early(x_ref, cot_ref, gate_w, down_w, gs_ref, logit_ref, gate_ref, hg_ref)

    items = {
        "up": {1: (1, 0, 2), 2: (1, 0, 2), 3: (1, 0, 2), 4: (0, 2)},
        "down": {1: (1, 0, 2), 2: (1, 0, 2), 3: (1, 0, 2), 4: (1,)},
    }
    for half in (1, 0):
        cp.wait_recv(("t", half))
        if half == 0:
            r_copy(("far", 0), own_slot, 0, far)
        r_copy(("up", 1, half), own_slot, half, up)
        r_copy(("down", 1, half), own_slot, half, down)
    r_copy(("far", 1), own_slot, 1, far)
    cp.wait_recv("near")
    for d in range(3):
        l_copy(("y", d, 1), col_of(1 - xl, 0, core), along[d])
    l_copy("sibnear", col_of(1 - xl, 0, core), sibling)
    cp.wait_recv(("far", 0))
    r_copy(("up", 1, 2), slot_of(1 - xh, 0), 0, up)
    r_copy(("down", 1, 2), slot_of(1 - xh, 0), 0, down)

    def hop(h):
        for item in (1, 0, 2):
            for flow, sign, device in (("up", -1, up), ("down", 1, down)):
                if item not in items[flow][h]:
                    continue
                cp.wait_recv((flow, h, item))
                slot = slot_of(1 - xh if item == 2 else xh, sign * h + 8)
                if h < 4 and item in items[flow][h + 1]:
                    r_copy((flow, h + 1, item), slot, item % 2, device)
                if item == 1:
                    r_copy(("cross", flow, h), slot, 1, far)

    def l_hop(part):
        for d in range(3):
            cp.wait_recv(("y", d, part))
            l_copy(("sib", d, part), col_of(1 - xl if part else xl, 3 - d, core), sibling)

    order = [0, 7, 1, 6, 2, 5, 3, 4]
    quads = [[slot_of(h, dz) for dz in order[2 * q : 2 * q + 2] for h in range(2)] for q in range(4)]

    def left(q):
        project(lpan, [col_at(slot) for slot in quads[q]], q, wa, sa, a_ref)

    def right(q):
        project(rpan, quads[q], q, wb, sb, b_ref)

    hop(1)
    l_hop(0)
    hop(2)
    l_hop(1)
    cp.wait_recv(("far", 1))
    cp.wait_recv(("cross", "up", 1))
    right(0)
    for name in ["sib", "sibnear"] + [("sib", d, part) for part in range(2) for d in range(3)]:
        cp.wait_recv(name)
    left(0)
    hop(3)
    cp.wait_recv(("cross", "down", 1))
    cp.wait_recv(("cross", "up", 2))
    right(1)
    left(1)
    left(2)
    hop(4)
    cp.wait_recv(("cross", "down", 2))
    cp.wait_recv(("cross", "up", 3))
    right(2)
    left(3)
    cp.wait_recv(("cross", "down", 3))
    cp.wait_recv(("cross", "down", 4))
    right(3)
    products(a_ref, b_ref, t_ref)
    turn(t_ref, tri, tri_l, tri_r)
    finish(x_ref, cot_ref, out_w, up_w, down_w, hs_ref, logit_ref, gate_ref, hg_ref, tri, tri_l, tri_r, out_ref, acc)

    total = acc[...]
    for stage, (group, place) in enumerate(((line, z * 2 + core), (plane, (xh * 2 + xl) * 4 + y))):
        slots[stage, place] = total
        ref = slots.at[stage, place]
        copies = []
        for n in range(1, 16):
            copy = pltpu.make_async_remote_copy(
                src_ref=ref,
                dst_ref=ref,
                send_sem=sum_send.at[stage, n],
                recv_sem=sum_recv.at[stage, n],
                device_id=group[n],
                device_id_type=MESH,
            )
            copy.start()
            copies.append(copy)
        for copy in copies:
            copy.wait_recv()
        total = jnp.sum(slots[stage], axis=0)
        for copy in copies:
            copy.wait_send()
    gate_out[...] = total[:3]
    hidden_out[...] = total[3:7]
    cp.wait_sends()
    assert cp.count == N_COPIES


VMEM = pl.BlockSpec(memory_space=pltpu.VMEM)
SMEM = pl.BlockSpec(memory_space=pltpu.SMEM)


def shards(pair_state, valid_tokens, proj_weight, gate_weight, out_weight, up_weight, down_weight, gate_scales, hidden_scales, cotangent):
    panel = pltpu.VMEM((16, BLK, BLK, C), BF16)
    edge = pltpu.VMEM((4, C * SA, 128), F32)
    positions = pltpu.VMEM((BLK * BLK, C), F32)
    layer_out, gate_grads, hidden_grads = pl.pallas_call(
        layer_kernel,
        out_shape=(
            jax.ShapeDtypeStruct((BLK, BLK, C), BF16),
            jax.ShapeDtypeStruct((3, C), F32),
            jax.ShapeDtypeStruct((4, C), F32),
        ),
        in_specs=[VMEM, SMEM] + [VMEM] * 8,
        out_specs=(VMEM, VMEM, VMEM),
        scratch_shapes=[
            panel, panel, edge, edge, pltpu.VMEM((C * ST, 128), F32), positions, positions, positions, positions, positions,
            pltpu.VMEM((BLK * BLK, 512), F32), pltpu.VMEM((8, C), F32),
            pltpu.VMEM((2 * C, C), BF16), pltpu.VMEM((2 * C, C), BF16), pltpu.VMEM((C, C), F32), pltpu.VMEM((C, C), F32),
            pltpu.VMEM((2, 16, 8, C), F32),
            pltpu.SemaphoreType.DMA((N_COPIES,)), pltpu.SemaphoreType.DMA((N_COPIES,)),
            pltpu.SemaphoreType.DMA((2, 16)), pltpu.SemaphoreType.DMA((2, 16)),
        ],
        compiler_params=pltpu.CompilerParams(collective_id=0, has_side_effects=True, vmem_limit_bytes=60 << 20),
        name="layer",
    )(pair_state, valid_tokens, proj_weight, gate_weight, out_weight, up_weight, down_weight, gate_scales, hidden_scales.reshape(1, 512), cotangent)
    return layer_out, gate_grads, hidden_grads.reshape(512)


def solution(mesh):
    return jax.shard_map(
        shards,
        mesh=mesh,
        in_specs=(P("row", "col", None), P(), P(), P(), P(), P(), P(), P(), P(), P("row", "col", None)),
        out_specs=(P("row", "col", None), P(), P()),
        check_vma=False,
    )
```

```python
import functools

import jax
import jax.numpy as jnp
from jax import lax
from jax.experimental import pallas as pl
from jax.experimental.pallas import tpu as pltpu
from jax.sharding import PartitionSpec as P

F32, BF16 = jnp.float32, jnp.bfloat16
EPS = 1e-5
MESH = pl.DeviceIdType.MESH
C = 128
BLK = 32
SA = 65
GROUP = 16
WIDE = 64
ST = 33


def mm(a, b):
    return jnp.dot(a, b, preferred_element_type=F32)


def mm_nt(a, b):
    return lax.dot_general(a, b, (((1,), (1,)), ((), ())), preferred_element_type=F32)


def sigmoid(v):
    return 0.5 * jnp.tanh(0.5 * v) + 0.5


def norm(v):
    centred = v - jnp.mean(v, axis=-1, keepdims=True)
    inverse = lax.rsqrt(jnp.mean(centred * centred, axis=-1, keepdims=True) + EPS)
    return centred * inverse, inverse


def norm_back(g, hat, inverse):
    g_mean = jnp.mean(g, axis=-1, keepdims=True)
    cross = jnp.mean(g * hat, axis=-1, keepdims=True)
    return inverse * (g - g_mean - hat * cross)


class Copies:
    def __init__(self, send, recv):
        self.send, self.recv, self.count, self.table = send, recv, 0, {}

    def start(self, name, src, dst, device, when=None):
        copy = pltpu.make_async_remote_copy(
            src_ref=src,
            dst_ref=dst,
            send_sem=self.send.at[self.count],
            recv_sem=self.recv.at[self.count],
            device_id=device,
            device_id_type=MESH,
        )
        self.count += 1
        self.table[name] = (copy, when)
        if when is None:
            copy.start()
        else:
            pl.when(when)(copy.start)

    def wait_recv(self, name):
        copy, when = self.table[name]
        if when is None:
            copy.wait_recv()
        else:
            pl.when(when)(copy.wait_recv)

    def wait_sends(self):
        for copy, when in self.table.values():
            if when is None:
                copy.wait_send()
            else:
                pl.when(when)(copy.wait_send)


PIECES = 4
CROSSING = (2, 3)
PIECE = BLK // PIECES
ITEMS = [(0, p) for p in CROSSING] + [(h, p) for h in range(2) for p in range(PIECES) if p not in CROSSING]
N_COPIES = 17 + 2 * PIECES + 7 * (len(ITEMS) + len(CROSSING))


def project(pan, blocks, quad, i, w_ref, s_ref, out):
    x = jnp.concatenate([pan[b, i + m] for m in range(GROUP) for b in blocks], axis=0)
    p = mm_nt(w_ref[...], x)
    for m in range(GROUP):
        value, logit = p[:C, m * 128 : (m + 1) * 128], p[C:, m * 128 : (m + 1) * 128]
        sig = 0.5 * jnp.tanh(s_ref[...] * logit) + 0.5
        proj = sig * value
        slope = proj * (logit * (1.0 - sig))
        out[quad, pl.ds(i + m, C, stride=SA), :] = proj
        out[quad, pl.ds(i + m + BLK, C, stride=SA), :] = slope


def products(a_ref, b_ref, t_ref, quads, first, last):
    def step(n, carry):
        for m in range(WIDE):
            ch = n * WIDE + m
            rows = pl.ds(ch * SA, 2 * BLK)
            a = jnp.concatenate([a_ref[q, rows, :].astype(BF16) for q in quads], axis=1)
            b = jnp.concatenate([b_ref[q, rows, :].astype(BF16) for q in quads], axis=1)
            t = mm_nt(a, b)
            t = jnp.concatenate([t[:BLK], t[BLK:]], axis=1)
            here = pl.ds(ch * ST, BLK)
            t_ref[here, :] = t if 0 in quads else t_ref[here, :] + t
        return carry

    lax.fori_loop(first, last, step, 0)


N_ROWS = 8
N_POS = N_ROWS * BLK


def parts_of(n):
    return pl.ds(n * N_ROWS, N_ROWS), pl.ds(pl.multiple_of(n * N_POS, N_POS), N_POS)


def early(x_ref, cot_ref, gate_w, down_w, gs_ref, logit_ref, gate_ref, hg_ref):
    gs = gs_ref[2:3, :]

    def chunk(n, carry):
        own, rows = parts_of(n)
        x = x_ref[own].reshape(N_POS, C).astype(F32)
        gate_logit = mm(norm(x)[0].astype(BF16), gate_w[...])
        logit_ref[rows, :] = gate_logit
        gate_ref[rows, :] = sigmoid(gs * gate_logit)
        hg_ref[rows, :] = mm_nt(cot_ref[own].reshape(N_POS, C), down_w[...])
        return carry

    lax.fori_loop(0, BLK // N_ROWS, chunk, 0)


def turn(t_ref, tri, tri_l, tri_r):
    def step(n, carry):
        for m in range(4):
            i = n * 4 + m
            t = t_ref[pl.ds(i, C, stride=ST), :].T
            rows = pl.ds(pl.multiple_of(i * BLK, BLK), BLK)
            tri[rows, :] = t[:BLK]
            tri_r[rows, :] = t[BLK : 2 * BLK]
            tri_l[rows, :] = t[2 * BLK : 3 * BLK]
        return carry

    lax.fori_loop(0, BLK // 4, step, 0)


def finish(x_ref, cot_ref, out_w, up_w, down_w, hs_ref, logit_ref, gate_ref, hg_ref, tri, tri_l, tri_r, acc):
    hs = hs_ref[...]
    x = x_ref[...].reshape(BLK * BLK, C).astype(F32)
    cot = cot_ref[...].reshape(BLK * BLK, C).astype(F32)
    gate_logit, gate, hidden_grad = logit_ref[...], gate_ref[...], hg_ref[...]
    tri_hat, tri_inv = norm(tri[...])
    out_proj = mm(tri_hat.astype(BF16), out_w[...])
    middle = (x + gate * out_proj).astype(BF16)
    mid_hat, mid_inv = norm(middle.astype(F32))
    upward = mm(mid_hat.astype(BF16), up_w[...])
    first, second = upward[:, :512], upward[:, 512:]
    s = sigmoid(first)
    act = first * s
    product = act * second
    hidden_term = jnp.sum(hidden_grad * product, axis=0, keepdims=True)
    scaled = hidden_grad * hs
    g_first = scaled * second * s * (1.0 + first * (1.0 - s))
    g_second = scaled * act
    g_up = jnp.concatenate([g_first.astype(BF16), g_second.astype(BF16)], axis=1)
    g_mid = cot + norm_back(mm_nt(g_up, up_w[...]), mid_hat, mid_inv)
    gate_term = jnp.sum(g_mid * out_proj * gate * (1.0 - gate) * gate_logit, axis=0, keepdims=True)
    g_out = (g_mid * gate).astype(BF16)
    t_grad = norm_back(mm_nt(g_out, out_w[...]), tri_hat, tri_inv).astype(BF16).astype(F32)
    left_term = jnp.sum(t_grad * tri_l[...], axis=0, keepdims=True)
    right_term = jnp.sum(t_grad * tri_r[...], axis=0, keepdims=True)
    parts = [left_term, right_term, gate_term] + [hidden_term[:, m * C : (m + 1) * C] for m in range(4)]
    acc[...] = jnp.concatenate(parts + [jnp.zeros((1, C), F32)], axis=0)
    return acc[...], middle, (hs * product).astype(BF16)


def layer_kernel(
    x_ref, valid_ref, proj_w, gate_w, out_w, up_w, down_w, gs_ref, hs_ref, cot_ref,
    out_ref, gate_out, hidden_out,
    lpan, rpan, a_ref, b_ref, t_ref, tri, tri_l, tri_r, logit_ref, gate_ref, hg_ref, acc, wa, wb, sa, sb, slots, out_buf,
    send, recv, sum_send, sum_recv, out_sem,
):
    r, c = lax.axis_index("row"), lax.axis_index("col")
    xh, z = r // 8, r % 8
    xl, y, core = c // 8, (c // 2) % 4, c % 2

    def row_of(h, dz):
        return h * 8 + (z + dz) % 8

    def col_of(h, dy, k):
        return (h * 4 + (y + dy) % 4) * 2 + k

    def slot_of(h, dz):
        return h * 8 + (z + dz + 8 - c % 8) % 8

    def col_at(slot):
        return slot // 8 * 8 + (slot + 2 * (c % 2)) % 4 * 2 + slot % 8 // 4

    own_slot = slot_of(xh, 0)
    above = (y + 2 * (z % 2)) % 4 + 4 * core
    to = (xl * 8 + (z + above) % 8, r)
    sent_slot = xl * 8 + above
    source = (c, col_at(own_slot))
    off = jnp.logical_or(c != r, own_slot % 8 != sent_slot % 8)

    far = (row_of(1 - xh, 0), c)
    up, down = (row_of(xh, 1), c), (row_of(xh, 7), c)
    sibling = (r, col_of(xl, 0, 1 - core))
    near = (r, col_of(1 - xl, 0, core))
    forth, back = (r, col_of(xl, 1, core)), (r, col_of(xl, 3, core))
    line = [(row_of(xh, dz), col_of(xl, 0, (core + dk) % 2)) for dz in range(8) for dk in range(2)]
    plane = [
        (row_of((xh + dh) % 2, 0), col_of((xl + dl) % 2, dy, core))
        for dh in range(2) for dl in range(2) for dy in range(4)
    ]

    barrier = pltpu.get_barrier_semaphore()
    for device in line[1:] + plane[1:]:
        pl.semaphore_signal(barrier, inc=1, device_id=device, device_id_type=MESH)

    @pl.when(off)
    def _():
        pl.semaphore_signal(barrier, inc=1, device_id=source, device_id_type=MESH)

    limit = valid_ref[0]
    rows_i = lax.broadcasted_iota(jnp.int32, (BLK, BLK, C), 0) + r * BLK
    rows_k = lax.broadcasted_iota(jnp.int32, (BLK, BLK, C), 1) + c * BLK
    keep = jnp.where(jnp.maximum(rows_i, rows_k) < limit, 1.0, 0.0)
    normed = (norm(x_ref[...].astype(F32))[0] * keep).astype(BF16)
    lpan[c] = normed

    @pl.when(jnp.logical_not(off))
    def _():
        rpan[own_slot] = normed

    pl.semaphore_wait(barrier, 30 + jnp.where(off, 1, 0))

    cp = Copies(send, recv)

    def part(p):
        return pl.ds(p * PIECE, PIECE)

    def r_copy(name, slot, p, device):
        ref = rpan.at[slot, part(p)]
        cp.start(name, ref, ref, device)

    def l_copy(name, slot, device):
        ref = lpan.at[slot]
        cp.start(name, ref, ref, device)

    def l_out(k, slot):
        l_copy(("forth", k), slot, forth)
        l_copy(("back", k), slot, back)

    def l_start():
        l_copy("near", c, near)
        l_out(0, c)
        l_copy("sib", c, sibling)

    pieces = [p for h, p in ITEMS if h == 0]
    for p in pieces:
        cp.start(("t", p), lpan.at[c, part(p)], rpan.at[sent_slot, part(p)], to, off)
    l_start()

    for w_ref, s_ref, side in ((wa, sa, 0), (wb, sb, 1)):
        w_ref[:C, :] = proj_w[:, side * C : (side + 1) * C].T
        w_ref[C:, :] = proj_w[:, (side + 2) * C : (side + 3) * C].T
        s_ref[...] = jnp.broadcast_to(0.5 * gs_ref[side : side + 1, :], (C, C)).T

    def last_hop(flow):
        return ITEMS[0::2] if flow == "up" else ITEMS[1::2]

    for p in pieces:
        cp.wait_recv(("t", p))
        if p not in CROSSING:
            r_copy(("far", p), own_slot, p, far)
        r_copy(("up", 1, (0, p)), own_slot, p, up)
        r_copy(("down", 1, (0, p)), own_slot, p, down)
    for h, p in ITEMS:
        if h:
            cp.wait_recv(("far", p))
            r_copy(("up", 1, (1, p)), slot_of(1 - xh, 0), p, up)
            r_copy(("down", 1, (1, p)), slot_of(1 - xh, 0), p, down)

    def l_near():
        cp.wait_recv("near")
        slot = col_of(1 - xl, 0, core)
        l_out(1, slot)
        l_copy("sibnear", slot, sibling)

    l_near()

    def hop(n, beside=()):
        for place, item in enumerate(ITEMS):
            for job, arguments in beside[place] if beside else ():
                job(*arguments)
            h, p = item
            for flow, sign, device in (("up", -1, up), ("down", 1, down)):
                if n == 4 and item not in last_hop(flow):
                    continue
                cp.wait_recv((flow, n, item))
                slot = slot_of(1 - xh if h else xh, sign * n + 8)
                if n < 3 or n == 3 and item in last_hop(flow):
                    r_copy((flow, n + 1, item), slot, p, device)
                if p in CROSSING:
                    r_copy(("cross", flow, n, p), slot, p, far)

    def crossed(flow, n):
        for p in CROSSING:
            if n < 4 or (0, p) in last_hop(flow):
                cp.wait_recv(("cross", flow, n, p))

    tops = (pl.ds(0, BLK // 2), pl.ds(BLK // 2, BLK // 2))

    def l_one(k):
        for n, (flow, dy, device) in enumerate((("forth", 3, forth), ("back", 1, back))):
            cp.wait_recv((flow, k))
            slot = col_of(1 - xl if k else xl, dy, core)
            ref = lpan.at[slot, tops[n]]
            cp.start((flow, k, "on"), ref, ref, device)
            l_copy(("sib", flow, k), slot, sibling)

    def l_two(k):
        for flow in ("forth", "back"):
            cp.wait_recv((flow, k, "on"))
        l_copy(("sib", "both", k), col_of(1 - xl if k else xl, 2, core), sibling)

    def l_end():
        for name in ["sib", "sibnear"] + [("sib", flow, k) for k in range(2) for flow in ("forth", "back", "both")]:
            cp.wait_recv(name)

    order = [0, 7, 1, 6, 2, 5, 3, 4]
    quads = [[slot_of(h, dz) for dz in order[2 * q : 2 * q + 2] for h in range(2)] for q in range(4)]

    def left(q, half):
        project(lpan, [col_at(slot) for slot in quads[q]], q, half * GROUP, wa, sa, a_ref)

    def right(q, half):
        project(rpan, quads[q], q, half * GROUP, wb, sb, b_ref)

    def triangle(qs, first, last):
        products(a_ref, b_ref, t_ref, qs, first, last)

    early(x_ref, cot_ref, gate_w, down_w, gs_ref, logit_ref, gate_ref, hg_ref)
    hop(1)
    for p in CROSSING:
        r_copy(("far", p), own_slot, p, far)
    l_one(0)
    hop(2)
    for p in CROSSING:
        cp.wait_recv(("far", p))
    crossed("up", 1)
    l_one(1)
    l_two(0)
    hop(3, ([], [(right, (0, 0))], [(right, (0, 1))], [(l_two, (1,)), (l_end, ()), (left, (0, 0))], [(left, (0, 1))], [(left, (1, 0))]))
    crossed("down", 1)
    crossed("up", 2)
    hop(4, (
        [], [], [(right, (1, 0)), (right, (1, 1))], [(left, (1, 1)), (left, (2, 0))],
        [(left, (2, 1))], [(left, (3, 0))],
    ))
    left(3, 1)
    crossed("down", 2)
    crossed("up", 3)
    right(2, 0)
    right(2, 1)
    crossed("down", 3)
    crossed("up", 4)
    crossed("down", 4)
    right(3, 0)
    right(3, 1)
    triangle((0, 1, 2, 3), 0, 2)
    turn(t_ref, tri, tri_l, tri_r)
    total, middle, hidden = finish(
        x_ref, cot_ref, out_w, up_w, down_w, hs_ref, logit_ref, gate_ref, hg_ref, tri, tri_l, tri_r, acc
    )

    for stage, (group, place) in enumerate(((line, z * 2 + core), (plane, (xh * 2 + xl) * 4 + y))):
        slots[stage, place] = total
        ref = slots.at[stage, place]
        copies = []
        for n in range(1, 16):
            copy = pltpu.make_async_remote_copy(
                src_ref=ref,
                dst_ref=ref,
                send_sem=sum_send.at[stage, n],
                recv_sem=sum_recv.at[stage, n],
                device_id=group[n],
                device_id_type=MESH,
            )
            copy.start()
            copies.append(copy)
        if stage == 0:
            layer_out = middle.astype(F32) + mm(hidden, down_w[...])
            out_ref[...] = layer_out.astype(BF16).reshape(BLK, BLK, C)
        for copy in copies:
            copy.wait_recv()
        total = jnp.sum(slots[stage], axis=0)
        for copy in copies:
            copy.wait_send()
    gate_out[...] = total[:3]
    hidden_out[...] = total[3:7]
    cp.wait_sends()
    assert cp.count == N_COPIES


VMEM = pl.BlockSpec(memory_space=pltpu.VMEM)
SMEM = pl.BlockSpec(memory_space=pltpu.SMEM)


def shards(pair_state, valid_tokens, proj_weight, gate_weight, out_weight, up_weight, down_weight, gate_scales, hidden_scales, cotangent):
    panel = pltpu.VMEM((16, BLK, BLK, C), BF16)
    edge = pltpu.VMEM((4, C * SA, 128), F32)
    positions = pltpu.VMEM((BLK * BLK, C), F32)
    layer_out, gate_grads, hidden_grads = pl.pallas_call(
        layer_kernel,
        out_shape=(
            jax.ShapeDtypeStruct((BLK, BLK, C), BF16),
            jax.ShapeDtypeStruct((3, C), F32),
            jax.ShapeDtypeStruct((4, C), F32),
        ),
        in_specs=[VMEM, SMEM] + [VMEM] * 8,
        out_specs=(VMEM, VMEM, VMEM),
        scratch_shapes=[
            panel, panel, edge, edge, pltpu.VMEM((C * ST, 128), F32), positions, positions, positions, positions, positions,
            pltpu.VMEM((BLK * BLK, 512), F32), pltpu.VMEM((8, C), F32),
            pltpu.VMEM((2 * C, C), BF16), pltpu.VMEM((2 * C, C), BF16), pltpu.VMEM((C, C), F32), pltpu.VMEM((C, C), F32),
            pltpu.VMEM((2, 16, 8, C), F32), pltpu.VMEM((BLK, BLK, C), BF16),
            pltpu.SemaphoreType.DMA((N_COPIES,)), pltpu.SemaphoreType.DMA((N_COPIES,)),
            pltpu.SemaphoreType.DMA((2, 16)), pltpu.SemaphoreType.DMA((2, 16)), pltpu.SemaphoreType.DMA,
        ],
        compiler_params=pltpu.CompilerParams(collective_id=0, has_side_effects=True, vmem_limit_bytes=60 << 20),
        name="layer",
    )(pair_state, valid_tokens, proj_weight, gate_weight, out_weight, up_weight, down_weight, gate_scales, hidden_scales.reshape(1, 512), cotangent)
    return layer_out, gate_grads, hidden_grads.reshape(512)


def solution(mesh):
    return jax.shard_map(
        shards,
        mesh=mesh,
        in_specs=(P("row", "col", None), P(), P(), P(), P(), P(), P(), P(), P(), P("row", "col", None)),
        out_specs=(P("row", "col", None), P(), P()),
        check_vma=False,
    )
```

```python
import functools

import jax
import jax.numpy as jnp
from jax import lax
from jax.experimental import pallas as pl
from jax.experimental.pallas import tpu as pltpu
from jax.sharding import PartitionSpec as P

F32, BF16 = jnp.float32, jnp.bfloat16
EPS = 1e-5
MESH = pl.DeviceIdType.MESH
C = 128
BLK = 32
SA = 65
GROUP = 16
WIDE = 64
ST = 33


def mm(a, b):
    return jnp.dot(a, b, preferred_element_type=F32)


def mm_nt(a, b):
    return lax.dot_general(a, b, (((1,), (1,)), ((), ())), preferred_element_type=F32)


def sigmoid(v):
    return 0.5 * jnp.tanh(0.5 * v) + 0.5


def norm(v):
    centred = v - jnp.mean(v, axis=-1, keepdims=True)
    inverse = lax.rsqrt(jnp.mean(centred * centred, axis=-1, keepdims=True) + EPS)
    return centred * inverse, inverse


def norm_back(g, hat, inverse):
    g_mean = jnp.mean(g, axis=-1, keepdims=True)
    cross = jnp.mean(g * hat, axis=-1, keepdims=True)
    return inverse * (g - g_mean - hat * cross)


FARTHEST = (
    (8, 9, 6, 7, 10, 11, 4, 5, 12, 13, 2, 3, 14, 15, 1),
    (10, 9, 11, 6, 14, 8, 5, 7, 13, 15, 2, 4, 12, 1, 3),
)


class Copies:
    def __init__(self, send, recv):
        self.send, self.recv, self.count, self.table = send, recv, 0, {}

    def start(self, name, src, dst, device, when=None):
        copy = pltpu.make_async_remote_copy(
            src_ref=src,
            dst_ref=dst,
            send_sem=self.send.at[self.count],
            recv_sem=self.recv.at[self.count],
            device_id=device,
            device_id_type=MESH,
        )
        self.count += 1
        self.table[name] = (copy, when)
        if when is None:
            copy.start()
        else:
            pl.when(when)(copy.start)

    def wait_recv(self, name):
        copy, when = self.table[name]
        if when is None:
            copy.wait_recv()
        else:
            pl.when(when)(copy.wait_recv)

    def wait_sends(self):
        for copy, when in self.table.values():
            if when is None:
                copy.wait_send()
            else:
                pl.when(when)(copy.wait_send)


PIECES = 4
CROSSING = (2, 3)
PIECE = BLK // PIECES
ITEMS = [(0, p) for p in CROSSING] + [(h, p) for h in range(2) for p in range(PIECES) if p not in CROSSING]
N_COPIES = 17 + 2 * PIECES + 7 * (len(ITEMS) + len(CROSSING))


def project(pan, blocks, quad, i, w_ref, s_ref, out):
    x = jnp.concatenate([pan[b, i + m] for m in range(GROUP) for b in blocks], axis=0)
    p = mm_nt(w_ref[...], x)
    for m in range(GROUP):
        value, logit = p[:C, m * 128 : (m + 1) * 128], p[C:, m * 128 : (m + 1) * 128]
        sig = 0.5 * jnp.tanh(s_ref[...] * logit) + 0.5
        proj = sig * value
        slope = proj * (logit * (1.0 - sig))
        out[quad, pl.ds(i + m, C, stride=SA), :] = proj
        out[quad, pl.ds(i + m + BLK, C, stride=SA), :] = slope


def products(a_ref, b_ref, t_ref, quads, first, last):
    def step(n, carry):
        for m in range(WIDE):
            ch = n * WIDE + m
            rows = pl.ds(ch * SA, 2 * BLK)
            a = jnp.concatenate([a_ref[q, rows, :].astype(BF16) for q in quads], axis=1)
            b = jnp.concatenate([b_ref[q, rows, :].astype(BF16) for q in quads], axis=1)
            t = mm_nt(a, b)
            t = jnp.concatenate([t[:BLK], t[BLK:]], axis=1)
            here = pl.ds(ch * ST, BLK)
            t_ref[here, :] = t if 0 in quads else t_ref[here, :] + t
        return carry

    lax.fori_loop(first, last, step, 0)


N_ROWS = 8
N_POS = N_ROWS * BLK


def parts_of(n):
    return pl.ds(n * N_ROWS, N_ROWS), pl.ds(pl.multiple_of(n * N_POS, N_POS), N_POS)


def early(x_ref, cot_ref, gate_w, down_w, gs_ref, logit_ref, gate_ref, hg_ref):
    gs = gs_ref[2:3, :]

    def chunk(n, carry):
        own, rows = parts_of(n)
        x = x_ref[own].reshape(N_POS, C).astype(F32)
        gate_logit = mm(norm(x)[0].astype(BF16), gate_w[...])
        logit_ref[rows, :] = gate_logit
        gate_ref[rows, :] = sigmoid(gs * gate_logit)
        hg_ref[rows, :] = mm_nt(cot_ref[own].reshape(N_POS, C), down_w[...])
        return carry

    lax.fori_loop(0, BLK // N_ROWS, chunk, 0)


def turn(t_ref, tri, tri_l, tri_r):
    def step(n, carry):
        for m in range(4):
            i = n * 4 + m
            t = t_ref[pl.ds(i, C, stride=ST), :].T
            rows = pl.ds(pl.multiple_of(i * BLK, BLK), BLK)
            tri[rows, :] = t[:BLK]
            tri_r[rows, :] = t[BLK : 2 * BLK]
            tri_l[rows, :] = t[2 * BLK : 3 * BLK]
        return carry

    lax.fori_loop(0, BLK // 4, step, 0)


def finish(x_ref, cot_ref, out_w, up_w, down_w, hs_ref, logit_ref, gate_ref, hg_ref, tri, tri_l, tri_r, acc):
    hs = hs_ref[...]
    x = x_ref[...].reshape(BLK * BLK, C).astype(F32)
    cot = cot_ref[...].reshape(BLK * BLK, C).astype(F32)
    gate_logit, gate, hidden_grad = logit_ref[...], gate_ref[...], hg_ref[...]
    tri_hat, tri_inv = norm(tri[...])
    out_proj = mm(tri_hat.astype(BF16), out_w[...])
    middle = (x + gate * out_proj).astype(BF16)
    mid_hat, mid_inv = norm(middle.astype(F32))
    upward = mm(mid_hat.astype(BF16), up_w[...])
    first, second = upward[:, :512], upward[:, 512:]
    s = sigmoid(first)
    act = first * s
    product = act * second
    hidden_term = jnp.sum(hidden_grad * product, axis=0, keepdims=True)
    scaled = hidden_grad * hs
    g_first = scaled * second * s * (1.0 + first * (1.0 - s))
    g_second = scaled * act
    g_up = jnp.concatenate([g_first.astype(BF16), g_second.astype(BF16)], axis=1)
    g_mid = cot + norm_back(mm_nt(g_up, up_w[...]), mid_hat, mid_inv)
    gate_term = jnp.sum(g_mid * out_proj * gate * (1.0 - gate) * gate_logit, axis=0, keepdims=True)
    g_out = (g_mid * gate).astype(BF16)
    t_grad = norm_back(mm_nt(g_out, out_w[...]), tri_hat, tri_inv).astype(BF16).astype(F32)
    left_term = jnp.sum(t_grad * tri_l[...], axis=0, keepdims=True)
    right_term = jnp.sum(t_grad * tri_r[...], axis=0, keepdims=True)
    parts = [left_term, right_term, gate_term] + [hidden_term[:, m * C : (m + 1) * C] for m in range(4)]
    acc[...] = jnp.concatenate(parts + [jnp.zeros((1, C), F32)], axis=0)
    return acc[...], middle, (hs * product).astype(BF16)


def layer_kernel(
    x_ref, valid_ref, proj_h, gate_h, out_h, up_h, down_h, gs_ref, hs_ref, cot_h,
    out_ref, gate_out, hidden_out,
    lpan, rpan, a_ref, b_ref, t_ref, tri, tri_l, tri_r, logit_ref, gate_ref, hg_ref, acc, wa, wb, sa, sb, slots, out_buf,
    proj_w, gate_w, out_w, up_w, down_w, cot_ref, load_sem,
    send, recv, sum_send, sum_recv, out_sem,
):
    r, c = lax.axis_index("row"), lax.axis_index("col")
    xh, z = r // 8, r % 8
    xl, y, core = c // 8, (c // 2) % 4, c % 2

    def row_of(h, dz):
        return h * 8 + (z + dz) % 8

    def col_of(h, dy, k):
        return (h * 4 + (y + dy) % 4) * 2 + k

    def slot_of(h, dz):
        return h * 8 + (z + dz + 8 - c % 8) % 8

    def col_at(slot):
        return slot // 8 * 8 + (slot + 2 * (c % 2)) % 4 * 2 + slot % 8 // 4

    own_slot = slot_of(xh, 0)
    above = (y + 2 * (z % 2)) % 4 + 4 * core
    to = (xl * 8 + (z + above) % 8, r)
    sent_slot = xl * 8 + above
    source = (c, col_at(own_slot))
    off = jnp.logical_or(c != r, own_slot % 8 != sent_slot % 8)

    far = (row_of(1 - xh, 0), c)
    up, down = (row_of(xh, 1), c), (row_of(xh, 7), c)
    sibling = (r, col_of(xl, 0, 1 - core))
    near = (r, col_of(1 - xl, 0, core))
    forth, back = (r, col_of(xl, 1, core)), (r, col_of(xl, 3, core))
    line = [(row_of(xh, dz), col_of(xl, 0, (core + dk) % 2)) for dz in range(8) for dk in range(2)]
    plane = [
        (row_of((xh + dh) % 2, 0), col_of((xl + dl) % 2, dy, core))
        for dh in range(2) for dl in range(2) for dy in range(4)
    ]

    loads = [
        pltpu.make_async_copy(src, dst, load_sem.at[n])
        for n, (src, dst) in enumerate(
            ((proj_h, proj_w), (gate_h, gate_w), (cot_h, cot_ref), (down_h, down_w), (out_h, out_w), (up_h, up_w))
        )
    ]
    for load in loads:
        load.start()

    barrier = pltpu.get_barrier_semaphore()
    for device in [line[n] for n in FARTHEST[0]] + [plane[n] for n in FARTHEST[1]]:
        pl.semaphore_signal(barrier, inc=1, device_id=device, device_id_type=MESH)

    @pl.when(off)
    def _():
        pl.semaphore_signal(barrier, inc=1, device_id=source, device_id_type=MESH)

    limit = valid_ref[0]
    rows_i = lax.broadcasted_iota(jnp.int32, (BLK, BLK, C), 0) + r * BLK
    rows_k = lax.broadcasted_iota(jnp.int32, (BLK, BLK, C), 1) + c * BLK
    keep = jnp.where(jnp.maximum(rows_i, rows_k) < limit, 1.0, 0.0)
    normed = (norm(x_ref[...].astype(F32))[0] * keep).astype(BF16)
    lpan[c] = normed

    @pl.when(jnp.logical_not(off))
    def _():
        rpan[own_slot] = normed

    pl.semaphore_wait(barrier, 30 + jnp.where(off, 1, 0))

    cp = Copies(send, recv)

    def part(p):
        return pl.ds(p * PIECE, PIECE)

    def r_copy(name, slot, p, device):
        ref = rpan.at[slot, part(p)]
        cp.start(name, ref, ref, device)

    def l_copy(name, slot, device):
        ref = lpan.at[slot]
        cp.start(name, ref, ref, device)

    def l_out(k, slot):
        l_copy(("forth", k), slot, forth)
        l_copy(("back", k), slot, back)

    def l_start():
        l_copy("near", c, near)
        l_out(0, c)
        l_copy("sib", c, sibling)

    pieces = [p for h, p in ITEMS if h == 0]
    for p in pieces:
        cp.start(("t", p), lpan.at[c, part(p)], rpan.at[sent_slot, part(p)], to, off)
    l_start()

    for load in loads:
        load.wait()
    for w_ref, s_ref, side in ((wa, sa, 0), (wb, sb, 1)):
        w_ref[:C, :] = proj_w[:, side * C : (side + 1) * C].T
        w_ref[C:, :] = proj_w[:, (side + 2) * C : (side + 3) * C].T
        s_ref[...] = jnp.broadcast_to(0.5 * gs_ref[side : side + 1, :], (C, C)).T

    def last_hop(flow):
        return ITEMS[0::2] if flow == "up" else ITEMS[1::2]

    for p in pieces:
        cp.wait_recv(("t", p))
        if p not in CROSSING:
            r_copy(("far", p), own_slot, p, far)
        r_copy(("up", 1, (0, p)), own_slot, p, up)
        r_copy(("down", 1, (0, p)), own_slot, p, down)
    for h, p in ITEMS:
        if h:
            cp.wait_recv(("far", p))
            r_copy(("up", 1, (1, p)), slot_of(1 - xh, 0), p, up)
            r_copy(("down", 1, (1, p)), slot_of(1 - xh, 0), p, down)

    def l_near():
        cp.wait_recv("near")
        slot = col_of(1 - xl, 0, core)
        l_out(1, slot)
        l_copy("sibnear", slot, sibling)

    l_near()

    def hop(n, beside=()):
        for place, item in enumerate(ITEMS):
            for job, arguments in beside[place] if beside else ():
                job(*arguments)
            h, p = item
            for flow, sign, device in (("up", -1, up), ("down", 1, down)):
                if n == 4 and item not in last_hop(flow):
                    continue
                cp.wait_recv((flow, n, item))
                slot = slot_of(1 - xh if h else xh, sign * n + 8)
                if n < 3 or n == 3 and item in last_hop(flow):
                    r_copy((flow, n + 1, item), slot, p, device)
                if p in CROSSING:
                    r_copy(("cross", flow, n, p), slot, p, far)

    def crossed(flow, n):
        for p in CROSSING:
            if n < 4 or (0, p) in last_hop(flow):
                cp.wait_recv(("cross", flow, n, p))

    tops = (pl.ds(0, BLK // 2), pl.ds(BLK // 2, BLK // 2))

    def l_one(k):
        for n, (flow, dy, device) in enumerate((("forth", 3, forth), ("back", 1, back))):
            cp.wait_recv((flow, k))
            slot = col_of(1 - xl if k else xl, dy, core)
            ref = lpan.at[slot, tops[n]]
            cp.start((flow, k, "on"), ref, ref, device)
            l_copy(("sib", flow, k), slot, sibling)

    def l_two(k):
        for flow in ("forth", "back"):
            cp.wait_recv((flow, k, "on"))
        l_copy(("sib", "both", k), col_of(1 - xl if k else xl, 2, core), sibling)

    def l_end():
        for name in ["sib", "sibnear"] + [("sib", flow, k) for k in range(2) for flow in ("forth", "back", "both")]:
            cp.wait_recv(name)

    order = [0, 7, 1, 6, 2, 5, 3, 4]
    quads = [[slot_of(h, dz) for dz in order[2 * q : 2 * q + 2] for h in range(2)] for q in range(4)]

    def left(q, half):
        project(lpan, [col_at(slot) for slot in quads[q]], q, half * GROUP, wa, sa, a_ref)

    def right(q, half):
        project(rpan, quads[q], q, half * GROUP, wb, sb, b_ref)

    def triangle(qs, first, last):
        products(a_ref, b_ref, t_ref, qs, first, last)

    early(x_ref, cot_ref, gate_w, down_w, gs_ref, logit_ref, gate_ref, hg_ref)
    hop(1)
    for p in CROSSING:
        r_copy(("far", p), own_slot, p, far)
    l_one(0)
    hop(2)
    for p in CROSSING:
        cp.wait_recv(("far", p))
    crossed("up", 1)
    l_one(1)
    l_two(0)
    hop(3, ([], [(right, (0, 0))], [(right, (0, 1))], [(l_two, (1,)), (l_end, ()), (left, (0, 0))], [(left, (0, 1))], [(left, (1, 0))]))
    crossed("down", 1)
    crossed("up", 2)
    hop(4, (
        [], [], [(right, (1, 0)), (right, (1, 1))], [(left, (1, 1)), (left, (2, 0))],
        [(left, (2, 1))], [(left, (3, 0))],
    ))
    left(3, 1)
    crossed("down", 2)
    crossed("up", 3)
    right(2, 0)
    right(2, 1)
    crossed("down", 3)
    crossed("up", 4)
    crossed("down", 4)
    right(3, 0)
    right(3, 1)
    triangle((0, 1, 2, 3), 0, 2)
    turn(t_ref, tri, tri_l, tri_r)
    total, middle, hidden = finish(
        x_ref, cot_ref, out_w, up_w, down_w, hs_ref, logit_ref, gate_ref, hg_ref, tri, tri_l, tri_r, acc
    )

    sent = []
    for stage, (group, place) in enumerate(((line, z * 2 + core), (plane, (xh * 2 + xl) * 4 + y))):
        slots[stage, place] = total
        ref = slots.at[stage, place]
        copies = []
        for n in FARTHEST[stage]:
            copy = pltpu.make_async_remote_copy(
                src_ref=ref,
                dst_ref=ref,
                send_sem=sum_send.at[stage, n],
                recv_sem=sum_recv.at[stage, n],
                device_id=group[n],
                device_id_type=MESH,
            )
            copy.start()
            copies.append(copy)
        if stage == 0:
            layer_out = middle.astype(F32) + mm(hidden, down_w[...])
            out_buf[...] = layer_out.astype(BF16).reshape(BLK, BLK, C)
            out_copy = pltpu.make_async_copy(out_buf, out_ref, load_sem.at[6])
            out_copy.start()
            cp.wait_sends()
        for copy in sent:
            copy.wait_send()
        for copy in copies:
            copy.wait_recv()
        total = jnp.sum(slots[stage], axis=0)
        sent = copies
    gate_out[...] = total[:3]
    hidden_out[...] = total[3:7]
    out_copy.wait()
    for copy in sent:
        copy.wait_send()
    assert cp.count == N_COPIES


VMEM = pl.BlockSpec(memory_space=pltpu.VMEM)
ANY = pl.BlockSpec(memory_space=pl.ANY)
SMEM = pl.BlockSpec(memory_space=pltpu.SMEM)


def hand_over(*refs):
    for src, dst in zip(refs[:3], refs[3:]):
        dst[...] = src[...]


def shards(pair_state, valid_tokens, proj_weight, gate_weight, out_weight, up_weight, down_weight, gate_scales, hidden_scales, cotangent):
    panel = pltpu.VMEM((16, BLK, BLK, C), BF16)
    edge = pltpu.VMEM((4, C * SA, 128), F32)
    positions = pltpu.VMEM((BLK * BLK, C), F32)
    layer_out, gate_grads, hidden_grads = pl.pallas_call(
        layer_kernel,
        out_shape=(
            jax.ShapeDtypeStruct((BLK, BLK, C), BF16),
            jax.ShapeDtypeStruct((3, C), F32),
            jax.ShapeDtypeStruct((4, C), F32),
        ),
        in_specs=[VMEM, SMEM] + [ANY] * 5 + [VMEM] * 2 + [ANY],
        out_specs=(ANY, VMEM, VMEM),
        scratch_shapes=[
            panel, panel, edge, edge, pltpu.VMEM((C * ST, 128), F32), positions, positions, positions, positions, positions,
            pltpu.VMEM((BLK * BLK, 512), F32), pltpu.VMEM((8, C), F32),
            pltpu.VMEM((2 * C, C), BF16), pltpu.VMEM((2 * C, C), BF16), pltpu.VMEM((C, C), F32), pltpu.VMEM((C, C), F32),
            pltpu.VMEM((2, 16, 8, C), F32), pltpu.VMEM((BLK, BLK, C), BF16),
            pltpu.VMEM((C, 4 * C), BF16), pltpu.VMEM((C, C), BF16), pltpu.VMEM((C, C), BF16), pltpu.VMEM((C, 1024), BF16),
            pltpu.VMEM((512, C), BF16), pltpu.VMEM((BLK, BLK, C), BF16), pltpu.SemaphoreType.DMA((7,)),
            pltpu.SemaphoreType.DMA((N_COPIES,)), pltpu.SemaphoreType.DMA((N_COPIES,)),
            pltpu.SemaphoreType.DMA((2, 16)), pltpu.SemaphoreType.DMA((2, 16)), pltpu.SemaphoreType.DMA,
        ],
        compiler_params=pltpu.CompilerParams(collective_id=0, has_side_effects=True, vmem_limit_bytes=60 << 20),
        name="layer",
    )(pair_state, valid_tokens, proj_weight, gate_weight, out_weight, up_weight, down_weight, gate_scales, hidden_scales.reshape(1, 512), cotangent)
    layer_out, gate_grads, hidden_grads = pl.pallas_call(
        hand_over,
        out_shape=tuple(jax.ShapeDtypeStruct(v.shape, v.dtype) for v in (layer_out, gate_grads, hidden_grads)),
        in_specs=[VMEM] * 3,
        out_specs=(VMEM,) * 3,
        name="hand_over",
    )(layer_out, gate_grads, hidden_grads)
    return layer_out, gate_grads, hidden_grads.reshape(512)


def solution(mesh):
    return jax.shard_map(
        shards,
        mesh=mesh,
        in_specs=(P("row", "col", None), P(), P(), P(), P(), P(), P(), P(), P(), P("row", "col", None)),
        out_specs=(P("row", "col", None), P(), P()),
        check_vma=False,
    )
```

```python
import functools

import jax
import jax.numpy as jnp
from jax import lax
from jax.experimental import pallas as pl
from jax.experimental.pallas import tpu as pltpu
from jax.sharding import PartitionSpec as P

F32, BF16 = jnp.float32, jnp.bfloat16
EPS = 1e-5
MESH = pl.DeviceIdType.MESH
C = 128
BLK = 32
SA = 65
GROUP = 16
WIDE = 64
ST = 33


def mm(a, b):
    return jnp.dot(a, b, preferred_element_type=F32)


def mm_nt(a, b):
    return lax.dot_general(a, b, (((1,), (1,)), ((), ())), preferred_element_type=F32)


def sigmoid(v):
    return 0.5 * jnp.tanh(0.5 * v) + 0.5


def norm(v):
    centred = v - jnp.mean(v, axis=-1, keepdims=True)
    inverse = lax.rsqrt(jnp.mean(centred * centred, axis=-1, keepdims=True) + EPS)
    return centred * inverse, inverse


def norm_back(g, hat, inverse):
    g_mean = jnp.mean(g, axis=-1, keepdims=True)
    cross = jnp.mean(g * hat, axis=-1, keepdims=True)
    return inverse * (g - g_mean - hat * cross)


FARTHEST = (
    (8, 9, 6, 7, 10, 11, 4, 5, 12, 13, 2, 3, 14, 15, 1),
    (10, 9, 11, 6, 14, 8, 5, 7, 13, 15, 2, 4, 12, 1, 3),
)


class Copies:
    def __init__(self, send, recv):
        self.send, self.recv, self.count, self.table = send, recv, 0, {}

    def start(self, name, src, dst, device, when=None):
        copy = pltpu.make_async_remote_copy(
            src_ref=src,
            dst_ref=dst,
            send_sem=self.send.at[self.count],
            recv_sem=self.recv.at[self.count],
            device_id=device,
            device_id_type=MESH,
        )
        self.count += 1
        self.table[name] = (copy, when)
        if when is None:
            copy.start()
        else:
            pl.when(when)(copy.start)

    def wait_recv(self, name):
        copy, when = self.table[name]
        if when is None:
            copy.wait_recv()
        else:
            pl.when(when)(copy.wait_recv)

    def wait_sends(self):
        for copy, when in self.table.values():
            if when is None:
                copy.wait_send()
            else:
                pl.when(when)(copy.wait_send)


PIECES = 4
CROSSING = (2, 3)
PIECE = BLK // PIECES
ITEMS = [(0, p) for p in CROSSING] + [(h, p) for h in range(2) for p in range(PIECES) if p not in CROSSING]
N_COPIES = 17 + 2 * PIECES + 7 * (len(ITEMS) + len(CROSSING))


def project(pan, blocks, quad, i, w_ref, s_ref, out):
    x = jnp.concatenate([pan[b, i + m] for m in range(GROUP) for b in blocks], axis=0)
    p = mm_nt(w_ref[...], x)
    for m in range(GROUP):
        value, logit = p[:C, m * 128 : (m + 1) * 128], p[C:, m * 128 : (m + 1) * 128]
        sig = 0.5 * jnp.tanh(s_ref[...] * logit) + 0.5
        proj = sig * value
        slope = proj * (logit * (1.0 - sig))
        out[quad, pl.ds(i + m, C, stride=SA), :] = proj
        out[quad, pl.ds(i + m + BLK, C, stride=SA), :] = slope


def products(a_ref, b_ref, t_ref, quads, first, last):
    def step(n, carry):
        for m in range(WIDE):
            ch = n * WIDE + m
            rows = pl.ds(ch * SA, 2 * BLK)
            a = jnp.concatenate([a_ref[q, rows, :].astype(BF16) for q in quads], axis=1)
            b = jnp.concatenate([b_ref[q, rows, :].astype(BF16) for q in quads], axis=1)
            t = mm_nt(a, b)
            t = jnp.concatenate([t[:BLK], t[BLK:]], axis=1)
            here = pl.ds(ch * ST, BLK)
            t_ref[here, :] = t if 0 in quads else t_ref[here, :] + t
        return carry

    lax.fori_loop(first, last, step, 0)


N_ROWS = 8
N_POS = N_ROWS * BLK


def parts_of(n):
    return pl.ds(n * N_ROWS, N_ROWS), pl.ds(pl.multiple_of(n * N_POS, N_POS), N_POS)


def early(x_ref, cot_ref, gate_w, down_w, gs_ref, logit_ref, gate_ref, hg_ref):
    gs = gs_ref[2:3, :]

    def chunk(n, carry):
        own, rows = parts_of(n)
        x = x_ref[own].reshape(N_POS, C).astype(F32)
        gate_logit = mm(norm(x)[0].astype(BF16), gate_w[...])
        logit_ref[rows, :] = gate_logit
        gate_ref[rows, :] = sigmoid(gs * gate_logit)
        hg_ref[rows, :] = mm_nt(cot_ref[own].reshape(N_POS, C), down_w[...])
        return carry

    lax.fori_loop(0, BLK // N_ROWS, chunk, 0)


def turn(t_ref, tri, tri_l, tri_r):
    def step(n, carry):
        for m in range(16):
            i = n * 16 + m
            t = t_ref[pl.ds(i, C, stride=ST), :].T
            rows = pl.ds(pl.multiple_of(i * BLK, BLK), BLK)
            tri[rows, :] = t[:BLK]
            tri_r[rows, :] = t[BLK : 2 * BLK]
            tri_l[rows, :] = t[2 * BLK : 3 * BLK]
        return carry

    lax.fori_loop(0, BLK // 16, step, 0)


def finish(x_ref, cot_ref, out_w, up_w, down_w, hs_ref, logit_ref, gate_ref, hg_ref, tri, tri_l, tri_r, acc):
    hs = hs_ref[...]
    x = x_ref[...].reshape(BLK * BLK, C).astype(F32)
    cot = cot_ref[...].reshape(BLK * BLK, C).astype(F32)
    gate_logit, gate, hidden_grad = logit_ref[...], gate_ref[...], hg_ref[...]
    tri_hat, tri_inv = norm(tri[...])
    out_proj = mm(tri_hat.astype(BF16), out_w[...])
    middle = (x + gate * out_proj).astype(BF16)
    mid_hat, mid_inv = norm(middle.astype(F32))
    upward = mm(mid_hat.astype(BF16), up_w[...])
    first, second = upward[:, :512], upward[:, 512:]
    s = sigmoid(first)
    act = first * s
    product = act * second
    hidden_term = jnp.sum(hidden_grad * product, axis=0, keepdims=True)
    scaled = hidden_grad * hs
    g_first = scaled * second * s * (1.0 + first * (1.0 - s))
    g_second = scaled * act
    g_up = jnp.concatenate([g_first.astype(BF16), g_second.astype(BF16)], axis=1)
    g_mid = cot + norm_back(mm_nt(g_up, up_w[...]), mid_hat, mid_inv)
    gate_term = jnp.sum(g_mid * out_proj * gate * (1.0 - gate) * gate_logit, axis=0, keepdims=True)
    g_out = (g_mid * gate).astype(BF16)
    t_grad = norm_back(mm_nt(g_out, out_w[...]), tri_hat, tri_inv).astype(BF16).astype(F32)
    left_term = jnp.sum(t_grad * tri_l[...], axis=0, keepdims=True)
    right_term = jnp.sum(t_grad * tri_r[...], axis=0, keepdims=True)
    parts = [left_term, right_term, gate_term] + [hidden_term[:, m * C : (m + 1) * C] for m in range(4)]
    acc[...] = jnp.concatenate(parts + [jnp.zeros((1, C), F32)], axis=0)
    return acc[...], middle, (hs * product).astype(BF16)


def layer_kernel(
    x_ref, valid_ref, proj_h, gate_h, out_h, up_h, down_h, gs_ref, hs_ref, cot_h,
    out_ref, gate_out, hidden_out,
    lpan, rpan, a_ref, b_ref, t_ref, tri, tri_l, tri_r, logit_ref, gate_ref, hg_ref, acc, wa, wb, sa, sb, slots, out_buf,
    proj_w, gate_w, out_w, up_w, down_w, cot_ref, load_sem,
    send, recv, sum_send, sum_recv, out_sem,
):
    r, c = lax.axis_index("row"), lax.axis_index("col")
    xh, z = r // 8, r % 8
    xl, y, core = c // 8, (c // 2) % 4, c % 2

    def row_of(h, dz):
        return h * 8 + (z + dz) % 8

    def col_of(h, dy, k):
        return (h * 4 + (y + dy) % 4) * 2 + k

    def slot_of(h, dz):
        return h * 8 + (z + dz + 8 - c % 8) % 8

    def col_at(slot):
        return slot // 8 * 8 + (slot + 2 * (c % 2)) % 4 * 2 + slot % 8 // 4

    own_slot = slot_of(xh, 0)
    above = (y + 2 * (z % 2)) % 4 + 4 * core
    to = (xl * 8 + (z + above) % 8, r)
    sent_slot = xl * 8 + above
    source = (c, col_at(own_slot))
    off = jnp.logical_or(c != r, own_slot % 8 != sent_slot % 8)

    far = (row_of(1 - xh, 0), c)
    up, down = (row_of(xh, 1), c), (row_of(xh, 7), c)
    sibling = (r, col_of(xl, 0, 1 - core))
    near = (r, col_of(1 - xl, 0, core))
    forth, back = (r, col_of(xl, 1, core)), (r, col_of(xl, 3, core))
    line = [(row_of(xh, dz), col_of(xl, 0, (core + dk) % 2)) for dz in range(8) for dk in range(2)]
    plane = [
        (row_of((xh + dh) % 2, 0), col_of((xl + dl) % 2, dy, core))
        for dh in range(2) for dl in range(2) for dy in range(4)
    ]

    loads = [
        pltpu.make_async_copy(src, dst, load_sem.at[n])
        for n, (src, dst) in enumerate(
            ((proj_h, proj_w), (gate_h, gate_w), (cot_h, cot_ref), (down_h, down_w), (out_h, out_w), (up_h, up_w))
        )
    ]
    for load in loads:
        load.start()

    barrier = pltpu.get_barrier_semaphore()
    for device in [line[n] for n in FARTHEST[0]] + [plane[n] for n in FARTHEST[1]]:
        pl.semaphore_signal(barrier, inc=1, device_id=device, device_id_type=MESH)

    @pl.when(off)
    def _():
        pl.semaphore_signal(barrier, inc=1, device_id=source, device_id_type=MESH)

    limit = valid_ref[0]
    rows_i = lax.broadcasted_iota(jnp.int32, (BLK, BLK, C), 0) + r * BLK
    rows_k = lax.broadcasted_iota(jnp.int32, (BLK, BLK, C), 1) + c * BLK
    keep = jnp.where(jnp.maximum(rows_i, rows_k) < limit, 1.0, 0.0)
    normed = (norm(x_ref[...].astype(F32))[0] * keep).astype(BF16)
    lpan[c] = normed

    @pl.when(jnp.logical_not(off))
    def _():
        rpan[own_slot] = normed

    pl.semaphore_wait(barrier, 30 + jnp.where(off, 1, 0))

    cp = Copies(send, recv)

    def part(p):
        return pl.ds(p * PIECE, PIECE)

    def r_copy(name, slot, p, device):
        ref = rpan.at[slot, part(p)]
        cp.start(name, ref, ref, device)

    def l_copy(name, slot, device):
        ref = lpan.at[slot]
        cp.start(name, ref, ref, device)

    def l_out(k, slot):
        l_copy(("forth", k), slot, forth)
        l_copy(("back", k), slot, back)

    def l_start():
        l_copy("near", c, near)
        l_out(0, c)
        l_copy("sib", c, sibling)

    pieces = [p for h, p in ITEMS if h == 0]
    for p in pieces:
        cp.start(("t", p), lpan.at[c, part(p)], rpan.at[sent_slot, part(p)], to, off)
    l_start()

    for load in loads:
        load.wait()
    for w_ref, s_ref, side in ((wa, sa, 0), (wb, sb, 1)):
        w_ref[:C, :] = proj_w[:, side * C : (side + 1) * C].T
        w_ref[C:, :] = proj_w[:, (side + 2) * C : (side + 3) * C].T
        s_ref[...] = jnp.broadcast_to(0.5 * gs_ref[side : side + 1, :], (C, C)).T

    def last_hop(flow):
        return ITEMS[0::2] if flow == "up" else ITEMS[1::2]

    for p in pieces:
        cp.wait_recv(("t", p))
        if p not in CROSSING:
            r_copy(("far", p), own_slot, p, far)
        r_copy(("up", 1, (0, p)), own_slot, p, up)
        r_copy(("down", 1, (0, p)), own_slot, p, down)
    for h, p in ITEMS:
        if h:
            cp.wait_recv(("far", p))
            r_copy(("up", 1, (1, p)), slot_of(1 - xh, 0), p, up)
            r_copy(("down", 1, (1, p)), slot_of(1 - xh, 0), p, down)

    def l_near():
        cp.wait_recv("near")
        slot = col_of(1 - xl, 0, core)
        l_out(1, slot)
        l_copy("sibnear", slot, sibling)

    l_near()

    def hop(n, beside=()):
        for place, item in enumerate(ITEMS):
            for job, arguments in beside[place] if beside else ():
                job(*arguments)
            h, p = item
            for flow, sign, device in (("up", -1, up), ("down", 1, down)):
                if n == 4 and item not in last_hop(flow):
                    continue
                cp.wait_recv((flow, n, item))
                slot = slot_of(1 - xh if h else xh, sign * n + 8)
                if n < 3 or n == 3 and item in last_hop(flow):
                    r_copy((flow, n + 1, item), slot, p, device)
                if p in CROSSING:
                    r_copy(("cross", flow, n, p), slot, p, far)

    def crossed(flow, n):
        for p in CROSSING:
            if n < 4 or (0, p) in last_hop(flow):
                cp.wait_recv(("cross", flow, n, p))

    tops = (pl.ds(0, BLK // 2), pl.ds(BLK // 2, BLK // 2))

    def l_one(k):
        for n, (flow, dy, device) in enumerate((("forth", 3, forth), ("back", 1, back))):
            cp.wait_recv((flow, k))
            slot = col_of(1 - xl if k else xl, dy, core)
            ref = lpan.at[slot, tops[n]]
            cp.start((flow, k, "on"), ref, ref, device)
            l_copy(("sib", flow, k), slot, sibling)

    def l_two(k):
        for flow in ("forth", "back"):
            cp.wait_recv((flow, k, "on"))
        l_copy(("sib", "both", k), col_of(1 - xl if k else xl, 2, core), sibling)

    def l_end():
        for name in ["sib", "sibnear"] + [("sib", flow, k) for k in range(2) for flow in ("forth", "back", "both")]:
            cp.wait_recv(name)

    order = [0, 7, 1, 6, 2, 5, 3, 4]
    quads = [[slot_of(h, dz) for dz in order[2 * q : 2 * q + 2] for h in range(2)] for q in range(4)]

    def left(q, half):
        project(lpan, [col_at(slot) for slot in quads[q]], q, half * GROUP, wa, sa, a_ref)

    def right(q, half):
        project(rpan, quads[q], q, half * GROUP, wb, sb, b_ref)

    def triangle(qs, first, last):
        products(a_ref, b_ref, t_ref, qs, first, last)

    early(x_ref, cot_ref, gate_w, down_w, gs_ref, logit_ref, gate_ref, hg_ref)
    hop(1)
    for p in CROSSING:
        r_copy(("far", p), own_slot, p, far)
    l_one(0)
    hop(2)
    for p in CROSSING:
        cp.wait_recv(("far", p))
    crossed("up", 1)
    l_one(1)
    l_two(0)
    hop(3, ([], [(right, (0, 0))], [(right, (0, 1))], [(l_two, (1,)), (l_end, ()), (left, (0, 0))], [(left, (0, 1))], [(left, (1, 0))]))
    crossed("down", 1)
    crossed("up", 2)
    hop(4, (
        [], [], [(right, (1, 0)), (right, (1, 1))], [(left, (1, 1)), (left, (2, 0))],
        [(left, (2, 1))], [(left, (3, 0))],
    ))
    left(3, 1)
    crossed("down", 2)
    crossed("up", 3)
    right(2, 0)
    right(2, 1)
    crossed("down", 3)
    crossed("up", 4)
    crossed("down", 4)
    right(3, 0)
    right(3, 1)
    triangle((0, 1, 2, 3), 0, 2)
    turn(t_ref, tri, tri_l, tri_r)
    total, middle, hidden = finish(
        x_ref, cot_ref, out_w, up_w, down_w, hs_ref, logit_ref, gate_ref, hg_ref, tri, tri_l, tri_r, acc
    )

    sent = []
    for stage, (group, place) in enumerate(((line, z * 2 + core), (plane, (xh * 2 + xl) * 4 + y))):
        slots[stage, place] = total
        ref = slots.at[stage, place]
        copies = []
        for n in FARTHEST[stage]:
            copy = pltpu.make_async_remote_copy(
                src_ref=ref,
                dst_ref=ref,
                send_sem=sum_send.at[stage, n],
                recv_sem=sum_recv.at[stage, n],
                device_id=group[n],
                device_id_type=MESH,
            )
            copy.start()
            copies.append(copy)
        if stage == 0:
            layer_out = middle.astype(F32) + mm(hidden, down_w[...])
            out_buf[...] = layer_out.astype(BF16).reshape(BLK, BLK, C)
            out_copy = pltpu.make_async_copy(out_buf, out_ref, load_sem.at[6])
            out_copy.start()
            cp.wait_sends()
        for copy in sent:
            copy.wait_send()
        for copy in copies:
            copy.wait_recv()
        total = jnp.sum(slots[stage], axis=0)
        sent = copies
    gate_out[...] = total[:3]
    hidden_out[...] = total[3:7]
    out_copy.wait()
    for copy in sent:
        copy.wait_send()
    assert cp.count == N_COPIES


VMEM = pl.BlockSpec(memory_space=pltpu.VMEM)
ANY = pl.BlockSpec(memory_space=pl.ANY)
SMEM = pl.BlockSpec(memory_space=pltpu.SMEM)


def hand_over(*refs):
    for src, dst in zip(refs[:3], refs[3:]):
        dst[...] = src[...]


def shards(pair_state, valid_tokens, proj_weight, gate_weight, out_weight, up_weight, down_weight, gate_scales, hidden_scales, cotangent):
    panel = pltpu.VMEM((16, BLK, BLK, C), BF16)
    edge = pltpu.VMEM((4, C * SA, 128), F32)
    positions = pltpu.VMEM((BLK * BLK, C), F32)
    layer_out, gate_grads, hidden_grads = pl.pallas_call(
        layer_kernel,
        out_shape=(
            jax.ShapeDtypeStruct((BLK, BLK, C), BF16),
            jax.ShapeDtypeStruct((3, C), F32),
            jax.ShapeDtypeStruct((4, C), F32),
        ),
        in_specs=[VMEM, SMEM] + [ANY] * 5 + [VMEM] * 2 + [ANY],
        out_specs=(ANY, VMEM, VMEM),
        scratch_shapes=[
            panel, panel, edge, edge, pltpu.VMEM((C * ST, 128), F32), positions, positions, positions, positions, positions,
            pltpu.VMEM((BLK * BLK, 512), F32), pltpu.VMEM((8, C), F32),
            pltpu.VMEM((2 * C, C), BF16), pltpu.VMEM((2 * C, C), BF16), pltpu.VMEM((C, C), F32), pltpu.VMEM((C, C), F32),
            pltpu.VMEM((2, 16, 8, C), F32), pltpu.VMEM((BLK, BLK, C), BF16),
            pltpu.VMEM((C, 4 * C), BF16), pltpu.VMEM((C, C), BF16), pltpu.VMEM((C, C), BF16), pltpu.VMEM((C, 1024), BF16),
            pltpu.VMEM((512, C), BF16), pltpu.VMEM((BLK, BLK, C), BF16), pltpu.SemaphoreType.DMA((7,)),
            pltpu.SemaphoreType.DMA((N_COPIES,)), pltpu.SemaphoreType.DMA((N_COPIES,)),
            pltpu.SemaphoreType.DMA((2, 16)), pltpu.SemaphoreType.DMA((2, 16)), pltpu.SemaphoreType.DMA,
        ],
        compiler_params=pltpu.CompilerParams(collective_id=0, has_side_effects=True, vmem_limit_bytes=60 << 20),
        name="layer",
    )(pair_state, valid_tokens, proj_weight, gate_weight, out_weight, up_weight, down_weight, gate_scales, hidden_scales.reshape(1, 512), cotangent)
    layer_out, gate_grads, hidden_grads = pl.pallas_call(
        hand_over,
        out_shape=tuple(jax.ShapeDtypeStruct(v.shape, v.dtype) for v in (layer_out, gate_grads, hidden_grads)),
        in_specs=[VMEM] * 3,
        out_specs=(VMEM,) * 3,
        name="hand_over",
    )(layer_out, gate_grads, hidden_grads)
    return layer_out, gate_grads, hidden_grads.reshape(512)


def solution(mesh):
    return jax.shard_map(
        shards,
        mesh=mesh,
        in_specs=(P("row", "col", None), P(), P(), P(), P(), P(), P(), P(), P(), P("row", "col", None)),
        out_specs=(P("row", "col", None), P(), P()),
        check_vma=False,
    )
```
